32 devices in a mesh: ctx: 8 (over z, y), tp: 4 (over x, core).
Axes of the slice: x: 2, y: 2, z: 4, core: 2. Of those that a mesh axis runs over, the one named last changes fastest.
Arguments:
- ssm_inputs: bfloat16 [2048, 8192], P('ctx', 'tp'), may hold values from -4 to 4
- state_maps: bfloat16 [2048, 8, 256], P('ctx', 'tp'), may hold values from -4 to 4
- ssm_gates: bfloat16 [2048, 8192], P('ctx', 'tp'), may hold values from -4 to 4
- time_steps: float32 [128, 2048], P('tp', 'ctx'), may hold values from -5 to 128
- log_rates: float32 [128], P('tp'), may hold values from -12 to 1
- skip_gain: float32 [128], P('tp'), may hold values from 0.5 to 2
- conv_inputs: bfloat16 [4, 8192], P(None, 'tp'), may hold values from -3 to 3
- conv_maps: bfloat16 [4, 8, 256], P(None, 'tp'), may hold values from -3 to 3
- norm_gain: float32 [8192], P('tp'), may hold values from 0.1 to 1.9
- out_weight: bfloat16 [8192, 4096], P('tp'), may hold values from -0.0625 to 0.0625
- queries: bfloat16 [2048, 8192], P('ctx', 'tp'), may hold values from -5 to 5
- attention_keys: bfloat16 [2048, 1024], P('ctx', 'tp'), may hold values from -5 to 5
- values: bfloat16 [2048, 1024], P('ctx', 'tp'), may hold values from -4 to 4
Outputs:
- ssm_out: bfloat16 [2048, 4096], P(('ctx', 'tp'))
- attn_out: bfloat16 [2048, 8192], P('ctx', 'tp')
The draws below stay inside these ranges and needn't reach their ends.
All inputs are finite; a program needn't handle non-finite values.
Results may differ from the reference program's by a relative error of at most 0.03.
Values may be sent and summed in bfloat16 or wider, within the bound.
A program may use at most 128 MiB of HBM per device.

```python
import math
import jax
import jax.numpy as jnp
from jax import lax

SPACE_HEADS = 128
SSM_DIM = 64
NSTATE = 128
GROUPS = 8
QUERY_HEADS = 64
KEY_VALUE_HEADS = 8
HEAD_SIZE = 128
DOUT = 4096
CONV = 4
TOK_DEV = 256
TOKEN_COUNT = 2048
N_TP = 4


def simple_jitter(key, shape):
    return jnp.clip(jax.random.normal(key, shape, jnp.float32), -4.0, 4.0)


def space_model_rule(key):
    slow_share = 0.5
    sluggish_heads = jax.random.uniform(jax.random.fold_in(key, 11), (SPACE_HEADS,), jnp.float32) < slow_share
    keep_share = jnp.exp(jax.random.uniform(jax.random.fold_in(key, 12), (SPACE_HEADS,), jnp.float32, math.log(0.2), math.log(0.8)))
    forget = jax.random.uniform(jax.random.fold_in(key, 13), (SPACE_HEADS,), jnp.float32, 30.0, 50.0)
    decline_rate = jnp.where(sluggish_heads, keep_share / (TOKEN_COUNT * 0.02), 1.0 / (forget * 0.02))
    spike_position = jax.random.randint(jax.random.fold_in(key, 14), (3,), 0, TOKEN_COUNT)
    spike_loss = jax.random.uniform(jax.random.fold_in(key, 15), (3, SPACE_HEADS), jnp.float32, 0.2, 0.4)
    return (sluggish_heads, decline_rate, spike_position, spike_loss)


def draw_log_rates(key, part):
    sluggish_heads, decline_rate, spike_position, spike_loss = space_model_rule(key)
    return jnp.log(decline_rate).astype(jnp.float32)


def draw_time_steps(key, part):
    sluggish_heads, decline_rate, spike_position, spike_loss = space_model_rule(key)
    base_step = jnp.exp(jax.random.uniform(jax.random.fold_in(key, 16), (SPACE_HEADS, TOKEN_COUNT), jnp.float32, math.log(0.01), math.log(0.04)))
    token_location = jnp.arange(TOKEN_COUNT)
    flagged = token_location[None, :] == spike_position[:, None]
    spike_step = -jnp.log1p(-spike_loss) / decline_rate[None, :]
    additional_step = jnp.sum(jnp.where(flagged[:, None, :], spike_step[:, :, None], 0.0), axis=0)
    any_flagged = jnp.any(flagged, axis=0)
    step_size = jnp.where(sluggish_heads[:, None] & any_flagged[None, :], additional_step, base_step)
    return (step_size + jnp.log(-jnp.expm1(-step_size))).astype(jnp.float32)


def draw_state_maps(key, part):
    sluggish_heads, decline_rate, spike_position, spike_loss = space_model_rule(key)
    random_jitter = simple_jitter(jax.random.fold_in(key, 17), (TOKEN_COUNT, GROUPS, 2 * NSTATE))
    token_location = jnp.arange(TOKEN_COUNT)
    any_flagged = jnp.any(token_location[None, :] == spike_position[:, None], axis=0)
    b_columns = jnp.arange(2 * NSTATE) < NSTATE
    shrink = jnp.where(any_flagged[:, None, None] & b_columns[None, None, :], 0.0001, 1.0)
    return (random_jitter * shrink).astype(jnp.bfloat16)


def draw_queries(key, part):
    random_jitter = simple_jitter(jax.random.fold_in(key, 1), (TOKEN_COUNT, QUERY_HEADS * HEAD_SIZE))
    return random_jitter.astype(jnp.bfloat16)


def draw_attention_keys(key, part):
    random_jitter = simple_jitter(jax.random.fold_in(key, 2), (TOKEN_COUNT, KEY_VALUE_HEADS * HEAD_SIZE))
    return random_jitter.astype(jnp.bfloat16)


def block_levels(stream_key, shape, shards, low, largest):
    level = 1.0
    for axis_at, shards_of in shards:
        heights = jax.random.uniform(jax.random.fold_in(jax.random.fold_in(stream_key, 6), axis_at), (shards_of,), jnp.float32, low / len(shards), largest / len(shards))
        level = level * jnp.repeat(jnp.exp(heights), shape[axis_at] // shards_of).reshape((-1,) + (1,) * (len(shape) - 1 - axis_at))
    return level


def bell_draw(stream_key, extent, spread, limit, cuts=(), kind=jnp.bfloat16):
    loudness = block_levels(stream_key, extent, cuts, -0.22, 0.18) if cuts else 1.0
    values = jax.random.normal(stream_key, extent, jnp.float32) * spread * loudness
    return jnp.minimum(jnp.maximum(values, -limit), limit).astype(kind)


def setup_inputs(seed: int = 0) -> dict:
    key_list = jax.random.split(jax.random.key(seed), 14)
    ssm_inputs = bell_draw(key_list[0], (TOKEN_COUNT, SPACE_HEADS * SSM_DIM), 1.0, 4.0, ((0, 8), (1, 4)))
    state_maps = draw_state_maps(jax.random.fold_in(key_list[13], 71), 0)
    ssm_gates = bell_draw(key_list[2], (TOKEN_COUNT, SPACE_HEADS * SSM_DIM), 1.0, 4.0, ((0, 8), (1, 4)))
    time_steps = draw_time_steps(jax.random.fold_in(key_list[13], 71), 0)
    log_rates = draw_log_rates(jax.random.fold_in(key_list[13], 71), 0)
    skip_gain = jnp.clip(0.5 + 1.5 * jax.random.uniform(key_list[5], (SPACE_HEADS,), jnp.float32) ** block_levels(key_list[5], (SPACE_HEADS,), ((0, 4),), -0.2, 0.2), 0.5, 2.0)
    conv_inputs = bell_draw(key_list[6], (CONV, SPACE_HEADS * SSM_DIM), CONV ** -0.5, 3.0, ((1, 4),))
    conv_maps = bell_draw(key_list[7], (CONV, GROUPS, 2 * NSTATE), CONV ** -0.5, 3.0, ((1, 4),))
    norm_gain = jnp.clip(1.0 + 0.18 * jax.random.normal(key_list[8], (SPACE_HEADS * SSM_DIM,), jnp.float32), 0.1, 1.9)
    out_weight = bell_draw(key_list[9], (SPACE_HEADS * SSM_DIM, DOUT), (SPACE_HEADS * SSM_DIM) ** -0.5, 0.0625, ((0, 4),))
    queries = draw_queries(jax.random.fold_in(key_list[13], 71), 0)
    attention_keys = draw_attention_keys(jax.random.fold_in(key_list[13], 71), 0)
    values = bell_draw(key_list[12], (TOKEN_COUNT, KEY_VALUE_HEADS * HEAD_SIZE), 1.0, 4.0, ((0, 8), (1, 4)))
    return {"ssm_inputs": ssm_inputs, "state_maps": state_maps, "ssm_gates": ssm_gates, "time_steps": time_steps, "log_rates": log_rates, "skip_gain": skip_gain, "conv_inputs": conv_inputs, "conv_maps": conv_maps, "norm_gain": norm_gain, "out_weight": out_weight, "queries": queries, "attention_keys": attention_keys, "values": values}


def conv_silu(series, conv_taps):
    tap_count = conv_taps.shape[0]
    length = series.shape[0]
    padded = jnp.concatenate([jnp.zeros((tap_count - 1,) + series.shape[1:], series.dtype), series], axis=0)
    summed = jnp.zeros(series.shape, jnp.float32)
    for tap_index in range(tap_count):
        summed = summed + conv_taps[tap_index].astype(jnp.float32) * padded[tap_index:tap_index + length].astype(jnp.float32)
    return lax.optimization_barrier(jax.nn.silu(summed).astype(jnp.bfloat16))

def mix_block(inputs_block, b_block, c_block, steps_block, decline_rate):
    tok_rows = inputs_block.shape[0]
    running_log = jnp.cumsum(steps_block * decline_rate[:, :, None], axis=2)
    map_products = jnp.einsum('tgn,sgn->gts', c_block.astype(jnp.float32), b_block.astype(jnp.float32))
    token_location = jnp.arange(tok_rows).astype(jnp.int32)
    causal = token_location[:, None] >= token_location[None, :]
    log_gap = running_log[:, :, :, None] - running_log[:, :, None, :]
    decay_table = jnp.where(causal, jnp.exp(jnp.minimum(log_gap, 0.0)), 0.0)
    mixer = lax.optimization_barrier((map_products[:, None] * decay_table * steps_block[:, :, None, :]).astype(jnp.bfloat16))
    inputs_float = inputs_block.astype(jnp.float32)
    inner_part = jnp.einsum('gjts,sgjp->tgjp', mixer.astype(jnp.float32), inputs_float)
    tail_weight = jnp.exp(running_log[:, :, -1:] - running_log) * steps_block
    weighted = lax.optimization_barrier((jnp.transpose(tail_weight, (2, 0, 1))[..., None] * inputs_float).astype(jnp.bfloat16))
    block_state = jnp.einsum('sgjp,sgn->gjpn', weighted.astype(jnp.float32), b_block.astype(jnp.float32))
    return (inner_part, block_state, running_log)

def attend(queries, attention_keys, values):
    shared_heads = QUERY_HEADS // KEY_VALUE_HEADS
    query_tile_block = min(512, TOKEN_COUNT)
    block_count = TOKEN_COUNT // query_tile_block
    score_scale = 1.0 / math.sqrt(HEAD_SIZE)
    pieces = []
    for current_block_index in range(block_count):
        upper_limit = (current_block_index + 1) * query_tile_block
        query_row_set = queries[current_block_index * query_tile_block:upper_limit].reshape(query_tile_block, KEY_VALUE_HEADS, shared_heads, HEAD_SIZE)
        key_head_rows = attention_keys[:upper_limit].reshape(upper_limit, KEY_VALUE_HEADS, HEAD_SIZE)
        value_head_rows = values[:upper_limit].reshape(upper_limit, KEY_VALUE_HEADS, HEAD_SIZE)
        query_pos = (current_block_index * query_tile_block + jnp.arange(query_tile_block)).astype(jnp.int32)
        key_pos = jnp.arange(upper_limit).astype(jnp.int32)
        allowed = key_pos[None, :] <= query_pos[:, None]

        def single_head(head_index):
            head_queries = lax.dynamic_index_in_dim(query_row_set, head_index, 1, keepdims=False)
            head_keys = lax.dynamic_index_in_dim(key_head_rows, head_index, 1, keepdims=False)
            head_values = lax.dynamic_index_in_dim(value_head_rows, head_index, 1, keepdims=False)
            scores = jnp.einsum('qrd,kd->rqk', head_queries.astype(jnp.float32), head_keys.astype(jnp.float32)) * score_scale
            scores = jnp.where(allowed[None], scores, -jnp.inf)
            row_peak = lax.optimization_barrier(jnp.max(scores, axis=2, keepdims=True))
            raised = jnp.exp(scores - row_peak)
            row_total = lax.optimization_barrier(jnp.sum(raised, axis=2))
            rounded = lax.optimization_barrier(raised.astype(jnp.bfloat16))
            summed = jnp.einsum('rqk,kd->qrd', rounded.astype(jnp.float32), head_values.astype(jnp.float32))
            return (summed / jnp.transpose(row_total)[..., None]).astype(jnp.bfloat16)
        head_outputs = lax.map(single_head, jnp.arange(KEY_VALUE_HEADS).astype(jnp.int32))
        pieces.append(jnp.transpose(head_outputs, (1, 0, 2, 3)).reshape(query_tile_block, QUERY_HEADS * HEAD_SIZE))
    return jnp.concatenate(pieces, axis=0)

def reference(ssm_inputs, state_maps, ssm_gates, time_steps, log_rates, skip_gain, conv_inputs, conv_maps, norm_gain, out_weight, queries, attention_keys, values):
    per_group = SPACE_HEADS // GROUPS
    block_count = TOKEN_COUNT // TOK_DEV
    mixed_inputs = conv_silu(ssm_inputs, conv_inputs).reshape(block_count, TOK_DEV, GROUPS, per_group, SSM_DIM)
    mixed_maps = conv_silu(state_maps, conv_maps).reshape(block_count, TOK_DEV, GROUPS, 2 * NSTATE)
    b_blocks = mixed_maps[..., :NSTATE]
    c_blocks = mixed_maps[..., NSTATE:]
    step_sizes = jnp.transpose(jax.nn.softplus(time_steps).reshape(GROUPS, per_group, block_count, TOK_DEV), (2, 0, 1, 3))
    decline_rate = -jnp.exp(log_rates).reshape(GROUPS, per_group)
    skip_part = skip_gain.reshape(GROUPS, per_group)[None, :, :, None]

    def advance(entering, blocks):
        inputs_block, b_block, c_block, steps_block = blocks
        inner_part, block_state, running_log = mix_block(inputs_block, b_block, c_block, steps_block, decline_rate)
        carried = jnp.einsum('tgn,gjpn->tgjp', c_block.astype(jnp.float32), entering, precision=lax.Precision.HIGHEST)
        outside = jnp.transpose(jnp.exp(running_log), (2, 0, 1))[..., None] * carried
        ssm_output = inner_part + outside + skip_part * inputs_block.astype(jnp.float32)
        leaving = jnp.exp(running_log[:, :, -1])[:, :, None, None] * entering + block_state
        return (leaving, ssm_output)
    start_state = jnp.zeros((GROUPS, per_group, SSM_DIM, NSTATE), jnp.float32)
    final_state, ssm_output = lax.scan(advance, start_state, (mixed_inputs, b_blocks, c_blocks, step_sizes))
    channel_count = per_group * SSM_DIM
    gated = ssm_output.reshape(TOKEN_COUNT, GROUPS, channel_count) * jax.nn.silu(ssm_gates.reshape(TOKEN_COUNT, GROUPS, channel_count).astype(jnp.float32))
    mean_square = lax.optimization_barrier(jnp.mean(gated * gated, axis=2, keepdims=True))
    normed = ((gated * lax.rsqrt(mean_square + 1e-05)).reshape(TOKEN_COUNT, SPACE_HEADS * SSM_DIM) * norm_gain).astype(jnp.bfloat16)
    slice_rows = SPACE_HEADS * SSM_DIM // N_TP
    ssm_sum = jnp.zeros((TOKEN_COUNT, DOUT), jnp.float32)
    for member in range(N_TP):
        partial_term = jnp.dot(normed[:, member * slice_rows:(member + 1) * slice_rows], out_weight[member * slice_rows:(member + 1) * slice_rows], preferred_element_type=jnp.float32)
        ssm_sum = ssm_sum + lax.optimization_barrier(partial_term.astype(jnp.bfloat16)).astype(jnp.float32)
    ssm_out = ssm_sum.astype(jnp.bfloat16)
    attn_out = attend(queries, attention_keys, values)
    return (ssm_out, attn_out)
```

```python
import functools

import jax
import jax.numpy as jnp
from jax import lax
from jax.experimental import pallas as pl
from jax.experimental.pallas import tpu as pltpu
from jax.sharding import PartitionSpec as P

HEAD_SIZE = 128
SHARED = 8
MESH = pl.DeviceIdType.MESH
LOG2E = 1.4426950408889634
BF = jnp.bfloat16
F32 = jnp.float32


def pair_lanes(col_a, col_b, rows, head_dim):
    lane = lax.broadcasted_iota(jnp.int32, (rows, 2 * head_dim), 1)
    return jnp.where(
        lane < head_dim,
        jnp.broadcast_to(col_a, (rows, 2 * head_dim)),
        jnp.broadcast_to(col_b, (rows, 2 * head_dim)),
    )


def silu(v):
    return v / (1.0 + jnp.exp(-v))


def exchange_kernel(
    n, inner, chunks, groups,
    x_ref, maps_ref, steps_ref, rates_ref, tapx_ref, tapm_ref, k_ref, v_ref,
    xc_ref, bc_ref, cum_ref, cumt_ref, dt_ref, ent_ref, kbuf, vbuf,
    halo_x, halo_m, ext, wbuf, srow, rrow, ein, eout, pbuf,
    halo_send, halo_recv, own_sem, kz_send, vz_send, kr_send, vr_send, k_recv, v_recv,
    s_send, s_recv, e_send, e_recv, p_send, p_recv,
):
    outer = n // inner
    c = lax.axis_index("ctx")
    hi = lax.div(c, inner)
    lo = lax.rem(c, inner)
    rows, xcols = x_ref.shape
    mcols = maps_ref.shape[1]
    heads = steps_ref.shape[0]
    head_dim = xcols // heads
    nstate = mcols // groups // 2
    width = srow.shape[3]
    part = width * chunks

    def remote(src, dst, send, recv, place):
        return pltpu.make_async_remote_copy(
            src_ref=src, dst_ref=dst, send_sem=send, recv_sem=recv,
            device_id={"ctx": place}, device_id_type=MESH,
        )

    barrier = pltpu.get_barrier_semaphore()
    for away in range(1, n):
        pl.semaphore_signal(
            barrier, inc=1, device_id={"ctx": lax.rem(c + away, n)}, device_id_type=MESH
        )
    pl.semaphore_wait(barrier, n - 1)

    up = lax.rem(c + inner, n)
    nxt = lax.rem(c + 1, n)

    def kv_up(src_k, src_v, block):
        return (
            remote(src_k, kbuf.at[block], kz_send.at[block], k_recv.at[block], up),
            remote(src_v, vbuf.at[block], vz_send.at[block], v_recv.at[block], up),
        )

    def kv_row(src_k, src_v, block, peer):
        place = hi * inner + peer
        return (
            remote(src_k, kbuf.at[block], kr_send.at[block, peer], k_recv.at[block], place),
            remote(src_v, vbuf.at[block], vr_send.at[block, peer], v_recv.at[block], place),
        )

    def halo_copies():
        return (
            remote(x_ref.at[pl.ds(rows - 16, 16)], halo_x, halo_send.at[0], halo_recv.at[0], nxt),
            remote(maps_ref.at[pl.ds(rows - 16, 16)], halo_m, halo_send.at[1], halo_recv.at[1], nxt),
        )

    @pl.when(c < n - 1)
    def _():
        for copy in halo_copies():
            copy.start()

    @pl.when(hi < outer - 1)
    def _():
        for copy in kv_up(k_ref, v_ref, c):
            copy.start()

    for away in range(1, inner):
        peer = lax.rem(lo + away, inner)

        @pl.when(peer > lo)
        def _():
            for copy in kv_row(k_ref, v_ref, c, peer):
                copy.start()

    own = (
        pltpu.make_async_copy(k_ref, kbuf.at[c], own_sem.at[0]),
        pltpu.make_async_copy(v_ref, vbuf.at[c], own_sem.at[1]),
    )
    for copy in own:
        copy.start()

    raw = steps_ref[...]
    dt = jnp.maximum(raw, 0.0) + jnp.log1p(jnp.exp(-jnp.abs(raw)))
    cum = dt * -jnp.exp(rates_ref[...])
    lane = lax.broadcasted_iota(jnp.int32, cum.shape, 1)
    reach = 1
    while reach < rows:
        cum = cum + jnp.where(lane >= reach, pltpu.roll(cum, reach, 1), 0.0)
        reach *= 2
    cum_ref[...] = cum
    dt_ref[...] = dt
    per_group = heads // groups
    last = cum[:, rows - 1 : rows]
    tail = (jnp.exp(last - cum) * dt).T
    cum_t = cum.T
    for g in range(groups):
        cumt_ref[g] = cum_t[:, g * per_group : (g + 1) * per_group]
    end_decay = jnp.exp(cum_t[rows - 1 : rows])

    @pl.when(c == 0)
    def _():
        halo_x[...] = jnp.zeros_like(halo_x)
        halo_m[...] = jnp.zeros_like(halo_m)

    @pl.when(c > 0)
    def _():
        for copy in halo_copies():
            copy.wait_recv()

    taps = tapx_ref.shape[0]
    step = 256

    def conv(src, halo, tap_ref, dst, cols):
        ext[0:8, :] = halo[:, cols].astype(F32)[8:16]
        ext[8 : 8 + rows, :] = src[:, cols].astype(F32)
        tap = tap_ref[:, cols].astype(F32)
        total = jnp.zeros((rows, step), F32)
        for k in range(taps):
            total = total + tap[k : k + 1] * ext[pl.ds(9 - taps + k, rows), :]
        dst[:, cols] = silu(total).astype(BF)

    for j in range(mcols // step):
        conv(maps_ref, halo_m, tapm_ref, bc_ref, slice(j * step, (j + 1) * step))
    for j in range(xcols // step):
        conv(x_ref, halo_x, tapx_ref, xc_ref, slice(j * step, (j + 1) * step))

    for p in range(heads // 2):
        cols = slice(2 * p * head_dim, 2 * (p + 1) * head_dim)
        weight = pair_lanes(
            tail[:, 2 * p : 2 * p + 1], tail[:, 2 * p + 1 : 2 * p + 2], rows, head_dim
        )
        wbuf[:, cols] = (weight * xc_ref[:, cols].astype(F32)).astype(BF)
        at = 2 * p * head_dim
        srow[at // part, (at % part) // width, nstate : nstate + 16,
             at % width : at % width + 2 * head_dim] = pair_lanes(
            end_decay[:, 2 * p : 2 * p + 1], end_decay[:, 2 * p + 1 : 2 * p + 2], 16, head_dim
        ).astype(BF)
    group_cols = xcols // groups
    for m in range(inner):
        for ch in range(chunks):
            at = m * part + ch * width
            g = at // group_cols
            b_map = bc_ref[:, g * 2 * nstate : g * 2 * nstate + nstate]
            srow[m, ch, 0:nstate] = lax.dot_general(
                b_map, wbuf[:, at : at + width], (((0,), (0,)), ((), ())),
                preferred_element_type=F32,
            ).astype(BF)

    def s_copy(peer, ch):
        return remote(
            srow.at[peer, ch], rrow.at[lo, ch], s_send.at[peer, ch], s_recv.at[lo, ch],
            hi * inner + peer,
        )

    def s_arrival(peer, ch):
        return remote(
            srow.at[peer, ch], rrow.at[peer, ch], s_send.at[peer, ch], s_recv.at[peer, ch],
            hi * inner + peer,
        )

    for ch in range(chunks):
        for away in range(1, inner):
            s_copy(lax.rem(lo + away, inner), ch).start()
        rrow[lo, ch] = srow[lo, ch]

    for k in range(1, outer):
        block = lax.rem(c - k * inner + n, n)

        @pl.when(hi >= k)
        def _():
            for copy in kv_up(kbuf.at[block], vbuf.at[block], block):
                copy.wait_recv()

            @pl.when(hi < outer - 1)
            def _():
                for copy in kv_up(kbuf.at[block], vbuf.at[block], block):
                    copy.start()

            for away in range(1, inner):
                for copy in kv_row(kbuf.at[block], vbuf.at[block], block, lax.rem(lo + away, inner)):
                    copy.start()

    def e_copy(ch):
        return remote(eout.at[ch], ein.at[ch], e_send.at[ch], e_recv.at[ch], up)

    def p_copy(peer, ch):
        return remote(
            pbuf.at[peer, ch], ent_ref.at[lo, ch], p_send.at[peer, ch], p_recv.at[lo, ch],
            hi * inner + peer,
        )

    def p_arrival(peer, ch):
        return remote(
            pbuf.at[peer, ch], ent_ref.at[peer, ch], p_send.at[peer, ch], p_recv.at[peer, ch],
            hi * inner + peer,
        )

    for ch in range(chunks):
        for away in range(1, inner):
            s_arrival(lax.rem(lo + away, inner), ch).wait_recv()

        @pl.when(hi == 0)
        def _():
            ein[ch] = jnp.zeros_like(ein[ch])

        @pl.when(hi > 0)
        def _():
            e_copy(ch).wait_recv()

        state = ein[ch].astype(F32)
        for m in range(inner):
            pbuf[m, ch] = state.astype(BF)
            state = rrow[m, ch, nstate : nstate + 16].astype(F32)[0:1] * state + rrow[
                m, ch, 0:nstate
            ].astype(F32)
        eout[ch] = state.astype(BF)

        @pl.when(hi < outer - 1)
        def _():
            e_copy(ch).start()

        for away in range(1, inner):
            p_copy(lax.rem(lo + away, inner), ch).start()
        ent_ref[lo, ch] = pbuf[lo, ch]

    for ch in range(chunks):
        for away in range(1, inner):
            p_arrival(lax.rem(lo + away, inner), ch).wait_recv()

    for k in range(outer):
        block = lax.rem(c - k * inner + n, n)
        for away in range(1, inner):
            peer = lax.rem(lo + away, inner)
            theirs = lax.rem(hi - k + outer, outer) * inner + peer

            @pl.when((hi >= k) if k else (peer < lo))
            def _():
                for copy in kv_row(kbuf.at[theirs], vbuf.at[theirs], theirs, peer):
                    copy.wait_recv()

            @pl.when((hi >= k) if k else (peer > lo))
            def _():
                for copy in kv_row(kbuf.at[block], vbuf.at[block], block, peer):
                    copy.wait_send()

        @pl.when((hi >= k) & (hi < outer - 1))
        def _():
            for copy in kv_up(kbuf.at[block], vbuf.at[block], block):
                copy.wait_send()

    for ch in range(chunks):
        for away in range(1, inner):
            peer = lax.rem(lo + away, inner)
            s_copy(peer, ch).wait_send()
            p_copy(peer, ch).wait_send()

        @pl.when(hi < outer - 1)
        def _():
            e_copy(ch).wait_send()

    @pl.when(c < n - 1)
    def _():
        for copy in halo_copies():
            copy.wait_send()

    for copy in own:
        copy.wait()


def exchange(n, groups, x, maps, steps, rates, tapx, tapm, keys, values):
    rows, xcols = x.shape
    mcols = maps.shape[1]
    heads = steps.shape[0]
    inner = 2 if n <= 8 else 8
    part = xcols // inner
    chunks = max(1, part // 512)
    width = part // chunks
    nstate = mcols // groups // 2
    vm = pl.BlockSpec(memory_space=pltpu.VMEM)
    hbm = pl.BlockSpec(memory_space=pl.ANY)
    dma = pltpu.SemaphoreType.DMA
    return pl.pallas_call(
        functools.partial(exchange_kernel, n, inner, chunks, groups),
        out_shape=(
            jax.ShapeDtypeStruct((rows, xcols), BF),
            jax.ShapeDtypeStruct((rows, mcols), BF),
            jax.ShapeDtypeStruct((heads, rows), F32),
            jax.ShapeDtypeStruct((groups, rows, heads // groups), F32),
            jax.ShapeDtypeStruct((heads, rows), F32),
            jax.ShapeDtypeStruct((inner, chunks, nstate, width), BF),
            jax.ShapeDtypeStruct((n,) + keys.shape, BF),
            jax.ShapeDtypeStruct((n,) + values.shape, BF),
        ),
        in_specs=[vm] * 6 + [hbm] * 2,
        out_specs=(vm,) * 6 + (hbm,) * 2,
        scratch_shapes=[
            pltpu.VMEM((16, xcols), BF),
            pltpu.VMEM((16, mcols), BF),
            pltpu.VMEM((rows + 8, 256), F32),
            pltpu.VMEM((rows, xcols), BF),
            pltpu.VMEM((inner, chunks, nstate + 16, width), BF),
            pltpu.VMEM((inner, chunks, nstate + 16, width), BF),
            pltpu.VMEM((chunks, nstate, width), BF),
            pltpu.VMEM((chunks, nstate, width), BF),
            pltpu.VMEM((inner, chunks, nstate, width), BF),
            dma((2,)), dma((2,)), dma((2,)),
            dma((n,)), dma((n,)), dma((n, inner)), dma((n, inner)), dma((n,)), dma((n,)),
            dma((inner, chunks)), dma((inner, chunks)),
            dma((chunks,)), dma((chunks,)),
            dma((inner, chunks)), dma((inner, chunks)),
        ],
        compiler_params=pltpu.CompilerParams(
            collective_id=0, has_side_effects=True, vmem_limit_bytes=40 * 2**20
        ),
        name="exchange",
    )(x, maps, steps, rates, tapx, tapm, keys, values)


def mixer_kernel(xc_ref, bc_ref, cum_ref, cumt_ref, dt_ref, ent_ref, z_ref, skip_ref, gain_ref,
                 out_ref, u_ref):
    rows, cols = xc_ref.shape
    per_group = cum_ref.shape[0]
    head_dim = cols // per_group
    nstate = bc_ref.shape[1] // 2
    width = ent_ref.shape[2]
    b_map = bc_ref[:, :nstate]
    c_map = bc_ref[:, nstate:]
    products = lax.dot_general(
        c_map, b_map, (((1,), (1,)), ((), ())), preferred_element_type=F32
    )
    tok = lax.broadcasted_iota(jnp.int32, (rows, rows), 0)
    src = lax.broadcasted_iota(jnp.int32, (rows, rows), 1)
    products = jnp.where(tok >= src, products, 0.0)
    cum_t = cumt_ref[0]
    rise = jnp.exp(cum_t)
    square = jnp.zeros((rows, 2 * head_dim), F32)
    lane = lax.broadcasted_iota(jnp.int32, (rows, 2 * head_dim), 1)
    for p in range(per_group // 2):
        at = 2 * p * head_dim
        span = slice(at, at + 2 * head_dim)
        xp = xc_ref[:, span]
        inner = []
        for h in (2 * p, 2 * p + 1):
            gap = jnp.minimum(cum_t[:, h : h + 1] - cum_ref[h : h + 1, :], 0.0)
            mix = (products * jnp.exp(gap) * dt_ref[h : h + 1, :]).astype(BF)
            inner.append(jnp.dot(mix, xp, preferred_element_type=F32))
        carried = jnp.dot(
            c_map, ent_ref[at // width, :, at % width : at % width + 2 * head_dim],
            preferred_element_type=F32,
        )
        xf = xp.astype(F32)
        y = (
            jnp.where(lane < head_dim, inner[0], inner[1])
            + pair_lanes(rise[:, 2 * p : 2 * p + 1], rise[:, 2 * p + 1 : 2 * p + 2], rows, head_dim)
            * carried
            + skip_ref[:, span] * xf
        )
        u = y * silu(z_ref[:, span].astype(F32))
        u_ref[:, span] = u
        square = square + u * u
    scale = lax.rsqrt(jnp.sum(square, axis=1, keepdims=True) * (1.0 / cols) + 1e-5)
    out_ref[...] = (u_ref[...] * scale * gain_ref[...]).astype(BF)


def mixer(groups, xc, bc, cum, cum_t, dt, ent, gates, skip, gain):
    rows, xcols = xc.shape
    cols = xcols // groups
    mcols = bc.shape[1] // groups
    per_group = cum.shape[0] // groups
    parts = ent.shape[0] // groups
    return pl.pallas_call(
        mixer_kernel,
        out_shape=jax.ShapeDtypeStruct((rows, xcols), BF),
        grid=(groups,),
        in_specs=[
            pl.BlockSpec((rows, cols), lambda g: (0, g)),
            pl.BlockSpec((rows, mcols), lambda g: (0, g)),
            pl.BlockSpec((per_group, rows), lambda g: (g, 0)),
            pl.BlockSpec((1, rows, per_group), lambda g: (g, 0, 0)),
            pl.BlockSpec((per_group, rows), lambda g: (g, 0)),
            pl.BlockSpec((parts,) + ent.shape[1:], lambda g: (g, 0, 0)),
            pl.BlockSpec((rows, cols), lambda g: (0, g)),
            pl.BlockSpec((1, cols), lambda g: (0, g)),
            pl.BlockSpec((1, cols), lambda g: (0, g)),
        ],
        out_specs=pl.BlockSpec((rows, cols), lambda g: (0, g)),
        scratch_shapes=[pltpu.VMEM((rows, cols), F32)],
        compiler_params=pltpu.CompilerParams(vmem_limit_bytes=40 * 2**20),
        cost_estimate=pl.CostEstimate(
            flops=2 * rows * rows * xcols * 2, bytes_accessed=6 * rows * xcols,
            transcendentals=cum.shape[0] * rows * rows,
        ),
        name="mixer",
    )(xc, bc, cum, cum_t, dt, ent, gates, skip, gain)


def attend_kernel(together, q_ref, k_ref, v_ref, o_ref, s_ref):
    c = lax.axis_index("ctx")
    rows = q_ref.shape[0]
    keys = k_ref.shape[1]
    q = jnp.concatenate(
        [q_ref[:, i * HEAD_SIZE : (i + 1) * HEAD_SIZE] for i in range(together)], axis=0
    )
    scale = HEAD_SIZE**-0.5 * LOG2E

    def score(j):
        return lax.dot_general(
            q, k_ref[j], (((1,), (1,)), ((), ())), preferred_element_type=F32
        ) * scale

    tok = lax.rem(lax.broadcasted_iota(jnp.int32, (together * rows, keys), 0), rows)
    pos = lax.broadcasted_iota(jnp.int32, (together * rows, keys), 1)
    own = jnp.where(pos <= tok, score(c), -1e30)
    s_ref[c] = own

    def first(j, peak):
        s = score(j)
        s_ref[j] = s
        return jnp.maximum(peak, s)

    peak = jnp.max(lax.fori_loop(0, c, first, own), axis=1, keepdims=True)

    def second(j, state):
        total, acc = state
        w = jnp.exp2(s_ref[j] - peak)
        return (
            total + w,
            acc + jnp.dot(w.astype(BF), v_ref[j], preferred_element_type=F32),
        )

    total, acc = lax.fori_loop(
        0, c + 1, second,
        (jnp.zeros((together * rows, keys), F32), jnp.zeros((together * rows, HEAD_SIZE), F32)),
    )
    out = (acc / jnp.sum(total, axis=1, keepdims=True)).astype(BF)
    for i in range(together):
        o_ref[:, i * HEAD_SIZE : (i + 1) * HEAD_SIZE] = out[i * rows : (i + 1) * rows]


def attend(queries, keys, values):
    rows, qcols = queries.shape
    n = keys.shape[0]
    together = 2
    steps = qcols // HEAD_SIZE // together
    per_kv = SHARED // together
    return pl.pallas_call(
        functools.partial(attend_kernel, together),
        out_shape=jax.ShapeDtypeStruct(queries.shape, BF),
        grid=(steps,),
        in_specs=[
            pl.BlockSpec((rows, together * HEAD_SIZE), lambda i: (0, i)),
            pl.BlockSpec((n, rows, HEAD_SIZE), lambda i: (0, 0, i // per_kv)),
            pl.BlockSpec((n, rows, HEAD_SIZE), lambda i: (0, 0, i // per_kv)),
        ],
        out_specs=pl.BlockSpec((rows, together * HEAD_SIZE), lambda i: (0, i)),
        scratch_shapes=[pltpu.VMEM((n, together * rows, rows), F32)],
        compiler_params=pltpu.CompilerParams(vmem_limit_bytes=48 * 2**20),
        cost_estimate=pl.CostEstimate(
            flops=4 * n * rows * rows * qcols, bytes_accessed=4 * rows * qcols,
            transcendentals=n * rows * rows * qcols // HEAD_SIZE,
        ),
        name="attend",
    )(queries, keys, values)


def per_device(
    n, ssm_inputs, state_maps, ssm_gates, time_steps, log_rates, skip_gain, conv_inputs, conv_maps,
    norm_gain, out_weight, queries, attention_keys, values,
):
    rows, xcols = ssm_inputs.shape
    groups = state_maps.shape[1]
    heads = log_rates.shape[0]
    xc, bc, cum, cum_t, dt, ent, kbuf, vbuf = exchange(
        n, groups, ssm_inputs, state_maps.reshape(rows, -1), time_steps,
        log_rates.reshape(heads, 1), conv_inputs, conv_maps.reshape(conv_maps.shape[0], -1),
        attention_keys, values,
    )
    skip = jnp.repeat(skip_gain, xcols // heads).reshape(1, xcols)
    normed = mixer(
        groups, xc, bc, cum, cum_t, dt, ent.reshape((-1,) + ent.shape[2:]), ssm_gates, skip,
        norm_gain.reshape(1, xcols),
    )
    ssm_out = lax.psum_scatter(
        jnp.dot(normed, out_weight, preferred_element_type=F32).astype(BF),
        "tp", scatter_dimension=0, tiled=True,
    )
    attn_out = attend(queries, kbuf, vbuf)
    return (ssm_out, attn_out)


def solution(mesh):
    placed = (
        P("ctx", "tp"),
        P("ctx", "tp", None),
        P("ctx", "tp"),
        P("tp", "ctx"),
        P("tp"),
        P("tp"),
        P(None, "tp"),
        P(None, "tp", None),
        P("tp"),
        P("tp", None),
        P("ctx", "tp"),
        P("ctx", "tp"),
        P("ctx", "tp"),
    )
    return jax.shard_map(
        functools.partial(per_device, mesh.shape["ctx"]),
        mesh=mesh,
        in_specs=placed,
        out_specs=(P(("ctx", "tp"), None), P("ctx", "tp")),
        check_vma=False,
    )
```

```python
import functools

import jax
import jax.numpy as jnp
from jax import lax
from jax.experimental import pallas as pl
from jax.experimental.pallas import tpu as pltpu
from jax.sharding import PartitionSpec as P

HEAD_SIZE = 128
SHARED = 8
MESH = pl.DeviceIdType.MESH
LOG2E = 1.4426950408889634
BF = jnp.bfloat16
F32 = jnp.float32


def pair_lanes(col_a, col_b, rows, head_dim):
    lane = lax.broadcasted_iota(jnp.int32, (rows, 2 * head_dim), 1)
    return jnp.where(
        lane < head_dim,
        jnp.broadcast_to(col_a, (rows, 2 * head_dim)),
        jnp.broadcast_to(col_b, (rows, 2 * head_dim)),
    )


def silu(v):
    return v / (1.0 + jnp.exp(-v))


def exchange_kernel(
    n, inner, chunks, groups,
    x_ref, maps_ref, steps_ref, rates_ref, tapx_ref, tapm_ref, k_ref, v_ref,
    xc_ref, bc_ref, cum_ref, cumt_ref, dt_ref, ent_ref, kbuf, vbuf,
    halo_x, halo_m, ext, wbuf, srow, rrow, ein, eout, pbuf,
    halo_send, halo_recv, own_sem, kz_send, vz_send, kr_send, vr_send, k_recv, v_recv,
    s_send, s_recv, e_send, e_recv, p_send, p_recv,
):
    outer = n // inner
    c = lax.axis_index("ctx")
    hi = lax.div(c, inner)
    lo = lax.rem(c, inner)
    rows, xcols = x_ref.shape
    mcols = maps_ref.shape[1]
    heads = steps_ref.shape[0]
    head_dim = xcols // heads
    nstate = mcols // groups // 2
    width = srow.shape[3]
    part = width * chunks

    def remote(src, dst, send, recv, place):
        return pltpu.make_async_remote_copy(
            src_ref=src, dst_ref=dst, send_sem=send, recv_sem=recv,
            device_id={"ctx": place}, device_id_type=MESH,
        )

    barrier = pltpu.get_barrier_semaphore()
    for away in range(1, n):
        pl.semaphore_signal(
            barrier, inc=1, device_id={"ctx": lax.rem(c + away, n)}, device_id_type=MESH
        )
    pl.semaphore_wait(barrier, n - 1)

    up = lax.rem(c + inner, n)
    nxt = lax.rem(c + 1, n)

    def kv_up(src_k, src_v, block):
        return (
            remote(src_k, kbuf.at[block], kz_send.at[block], k_recv.at[block], up),
            remote(src_v, vbuf.at[block], vz_send.at[block], v_recv.at[block], up),
        )

    def kv_row(src_k, src_v, block, peer):
        place = hi * inner + peer
        return (
            remote(src_k, kbuf.at[block], kr_send.at[block, peer], k_recv.at[block], place),
            remote(src_v, vbuf.at[block], vr_send.at[block, peer], v_recv.at[block], place),
        )

    def halo_copies():
        return (
            remote(x_ref.at[pl.ds(rows - 16, 16)], halo_x, halo_send.at[0], halo_recv.at[0], nxt),
            remote(maps_ref.at[pl.ds(rows - 16, 16)], halo_m, halo_send.at[1], halo_recv.at[1], nxt),
        )

    @pl.when(c < n - 1)
    def _():
        for copy in halo_copies():
            copy.start()

    @pl.when(hi < outer - 1)
    def _():
        for copy in kv_up(k_ref, v_ref, c):
            copy.start()

    for away in range(1, inner):
        peer = lax.rem(lo + away, inner)

        @pl.when(peer > lo)
        def _():
            for copy in kv_row(k_ref, v_ref, c, peer):
                copy.start()

    own = (
        pltpu.make_async_copy(k_ref, kbuf.at[c], own_sem.at[0]),
        pltpu.make_async_copy(v_ref, vbuf.at[c], own_sem.at[1]),
    )
    for copy in own:
        copy.start()

    raw = steps_ref[...]
    dt = jnp.maximum(raw, 0.0) + jnp.log1p(jnp.exp(-jnp.abs(raw)))
    cum = dt * -jnp.exp(rates_ref[...])
    lane = lax.broadcasted_iota(jnp.int32, cum.shape, 1)
    reach = 1
    while reach < rows:
        cum = cum + jnp.where(lane >= reach, pltpu.roll(cum, reach, 1), 0.0)
        reach *= 2
    cum_ref[...] = cum
    dt_ref[...] = dt
    per_group = heads // groups
    last = cum[:, rows - 1 : rows]
    tail = (jnp.exp(last - cum) * dt).T
    cum_t = cum.T
    for g in range(groups):
        cumt_ref[g] = cum_t[:, g * per_group : (g + 1) * per_group]
    end_decay = jnp.exp(cum_t[rows - 1 : rows])

    @pl.when(c == 0)
    def _():
        halo_x[...] = jnp.zeros_like(halo_x)
        halo_m[...] = jnp.zeros_like(halo_m)

    @pl.when(c > 0)
    def _():
        for copy in halo_copies():
            copy.wait_recv()

    taps = tapx_ref.shape[0]
    step = 256

    def conv(src, halo, tap_ref, dst, cols):
        ext[0:8, :] = halo[:, cols].astype(F32)[8:16]
        ext[8 : 8 + rows, :] = src[:, cols].astype(F32)
        tap = tap_ref[:, cols].astype(F32)
        total = jnp.zeros((rows, step), F32)
        for k in range(taps):
            total = total + tap[k : k + 1] * ext[pl.ds(9 - taps + k, rows), :]
        dst[:, cols] = silu(total).astype(BF)

    for j in range(mcols // step):
        conv(maps_ref, halo_m, tapm_ref, bc_ref, slice(j * step, (j + 1) * step))
    for j in range(xcols // step):
        conv(x_ref, halo_x, tapx_ref, xc_ref, slice(j * step, (j + 1) * step))

    for p in range(heads // 2):
        cols = slice(2 * p * head_dim, 2 * (p + 1) * head_dim)
        weight = pair_lanes(
            tail[:, 2 * p : 2 * p + 1], tail[:, 2 * p + 1 : 2 * p + 2], rows, head_dim
        )
        wbuf[:, cols] = (weight * xc_ref[:, cols].astype(F32)).astype(BF)
        at = 2 * p * head_dim
        srow[at // part, (at % part) // width, nstate : nstate + 16,
             at % width : at % width + 2 * head_dim] = pair_lanes(
            end_decay[:, 2 * p : 2 * p + 1], end_decay[:, 2 * p + 1 : 2 * p + 2], 16, head_dim
        ).astype(BF)
    group_cols = xcols // groups
    for m in range(inner):
        for ch in range(chunks):
            at = m * part + ch * width
            g = at // group_cols
            b_map = bc_ref[:, g * 2 * nstate : g * 2 * nstate + nstate]
            srow[m, ch, 0:nstate] = lax.dot_general(
                b_map, wbuf[:, at : at + width], (((0,), (0,)), ((), ())),
                preferred_element_type=F32,
            ).astype(BF)

    def s_copy(peer, ch):
        return remote(
            srow.at[peer, ch], rrow.at[lo, ch], s_send.at[peer, ch], s_recv.at[lo, ch],
            hi * inner + peer,
        )

    def s_arrival(peer, ch):
        return remote(
            srow.at[peer, ch], rrow.at[peer, ch], s_send.at[peer, ch], s_recv.at[peer, ch],
            hi * inner + peer,
        )

    for ch in range(chunks):
        for away in range(1, inner):
            s_copy(lax.rem(lo + away, inner), ch).start()
        rrow[lo, ch] = srow[lo, ch]

    for k in range(1, outer):
        block = lax.rem(c - k * inner + n, n)

        @pl.when(hi >= k)
        def _():
            for copy in kv_up(kbuf.at[block], vbuf.at[block], block):
                copy.wait_recv()

            @pl.when(hi < outer - 1)
            def _():
                for copy in kv_up(kbuf.at[block], vbuf.at[block], block):
                    copy.start()

            for away in range(1, inner):
                for copy in kv_row(kbuf.at[block], vbuf.at[block], block, lax.rem(lo + away, inner)):
                    copy.start()

    def e_copy(ch):
        return remote(eout.at[ch], ein.at[ch], e_send.at[ch], e_recv.at[ch], up)

    def p_copy(peer, ch):
        return remote(
            pbuf.at[peer, ch], ent_ref.at[lo, ch], p_send.at[peer, ch], p_recv.at[lo, ch],
            hi * inner + peer,
        )

    def p_arrival(peer, ch):
        return remote(
            pbuf.at[peer, ch], ent_ref.at[peer, ch], p_send.at[peer, ch], p_recv.at[peer, ch],
            hi * inner + peer,
        )

    for ch in range(chunks):
        for away in range(1, inner):
            s_arrival(lax.rem(lo + away, inner), ch).wait_recv()

        @pl.when(hi == 0)
        def _():
            ein[ch] = jnp.zeros_like(ein[ch])

        @pl.when(hi > 0)
        def _():
            e_copy(ch).wait_recv()

        state = ein[ch].astype(F32)
        for m in range(inner):
            pbuf[m, ch] = state.astype(BF)
            state = rrow[m, ch, nstate : nstate + 16].astype(F32)[0:1] * state + rrow[
                m, ch, 0:nstate
            ].astype(F32)
        eout[ch] = state.astype(BF)

        @pl.when(hi < outer - 1)
        def _():
            e_copy(ch).start()

        for away in range(1, inner):
            p_copy(lax.rem(lo + away, inner), ch).start()
        ent_ref[lo, ch] = pbuf[lo, ch]

    for ch in range(chunks):
        for away in range(1, inner):
            p_arrival(lax.rem(lo + away, inner), ch).wait_recv()

    for k in range(outer):
        block = lax.rem(c - k * inner + n, n)
        for away in range(1, inner):
            peer = lax.rem(lo + away, inner)
            theirs = lax.rem(hi - k + outer, outer) * inner + peer

            @pl.when((hi >= k) if k else (peer < lo))
            def _():
                for copy in kv_row(kbuf.at[theirs], vbuf.at[theirs], theirs, peer):
                    copy.wait_recv()

            @pl.when((hi >= k) if k else (peer > lo))
            def _():
                for copy in kv_row(kbuf.at[block], vbuf.at[block], block, peer):
                    copy.wait_send()

        @pl.when((hi >= k) & (hi < outer - 1))
        def _():
            for copy in kv_up(kbuf.at[block], vbuf.at[block], block):
                copy.wait_send()

    for ch in range(chunks):
        for away in range(1, inner):
            peer = lax.rem(lo + away, inner)
            s_copy(peer, ch).wait_send()
            p_copy(peer, ch).wait_send()

        @pl.when(hi < outer - 1)
        def _():
            e_copy(ch).wait_send()

    @pl.when(c < n - 1)
    def _():
        for copy in halo_copies():
            copy.wait_send()

    for copy in own:
        copy.wait()


def exchange(n, groups, x, maps, steps, rates, tapx, tapm, keys, values):
    rows, xcols = x.shape
    mcols = maps.shape[1]
    heads = steps.shape[0]
    inner = 2 if n <= 8 else 8
    part = xcols // inner
    chunks = max(1, part // 512)
    width = part // chunks
    nstate = mcols // groups // 2
    vm = pl.BlockSpec(memory_space=pltpu.VMEM)
    hbm = pl.BlockSpec(memory_space=pl.ANY)
    dma = pltpu.SemaphoreType.DMA
    return pl.pallas_call(
        functools.partial(exchange_kernel, n, inner, chunks, groups),
        out_shape=(
            jax.ShapeDtypeStruct((rows, xcols), BF),
            jax.ShapeDtypeStruct((rows, mcols), BF),
            jax.ShapeDtypeStruct((heads, rows), F32),
            jax.ShapeDtypeStruct((groups, rows, heads // groups), F32),
            jax.ShapeDtypeStruct((heads, rows), F32),
            jax.ShapeDtypeStruct((inner, chunks, nstate, width), BF),
            jax.ShapeDtypeStruct((n,) + keys.shape, BF),
            jax.ShapeDtypeStruct((n,) + values.shape, BF),
        ),
        in_specs=[vm] * 6 + [hbm] * 2,
        out_specs=(vm,) * 6 + (hbm,) * 2,
        scratch_shapes=[
            pltpu.VMEM((16, xcols), BF),
            pltpu.VMEM((16, mcols), BF),
            pltpu.VMEM((rows + 8, 256), F32),
            pltpu.VMEM((rows, xcols), BF),
            pltpu.VMEM((inner, chunks, nstate + 16, width), BF),
            pltpu.VMEM((inner, chunks, nstate + 16, width), BF),
            pltpu.VMEM((chunks, nstate, width), BF),
            pltpu.VMEM((chunks, nstate, width), BF),
            pltpu.VMEM((inner, chunks, nstate, width), BF),
            dma((2,)), dma((2,)), dma((2,)),
            dma((n,)), dma((n,)), dma((n, inner)), dma((n, inner)), dma((n,)), dma((n,)),
            dma((inner, chunks)), dma((inner, chunks)),
            dma((chunks,)), dma((chunks,)),
            dma((inner, chunks)), dma((inner, chunks)),
        ],
        compiler_params=pltpu.CompilerParams(
            collective_id=0, has_side_effects=True, vmem_limit_bytes=40 * 2**20
        ),
        name="exchange",
    )(x, maps, steps, rates, tapx, tapm, keys, values)


def mixer_kernel(xc_ref, bc_ref, cum_ref, cumt_ref, dt_ref, ent_ref, z_ref, skip_ref, gain_ref,
                 out_ref, u_ref):
    rows, cols = xc_ref.shape
    per_group = cum_ref.shape[0]
    head_dim = cols // per_group
    nstate = bc_ref.shape[1] // 2
    width = ent_ref.shape[2]
    b_map = bc_ref[:, :nstate]
    c_map = bc_ref[:, nstate:]
    products = lax.dot_general(
        c_map, b_map, (((1,), (1,)), ((), ())), preferred_element_type=F32
    )
    tok = lax.broadcasted_iota(jnp.int32, (rows, rows), 0)
    src = lax.broadcasted_iota(jnp.int32, (rows, rows), 1)
    products = jnp.where(tok >= src, products, 0.0)
    cum_t = cumt_ref[0]
    rise = jnp.exp(cum_t)
    square = jnp.zeros((rows, 2 * head_dim), F32)
    lane = lax.broadcasted_iota(jnp.int32, (rows, 2 * head_dim), 1)
    for p in range(per_group // 2):
        at = 2 * p * head_dim
        span = slice(at, at + 2 * head_dim)
        xp = xc_ref[:, span]
        inner = []
        for h in (2 * p, 2 * p + 1):
            gap = jnp.minimum(cum_t[:, h : h + 1] - cum_ref[h : h + 1, :], 0.0)
            mix = (products * jnp.exp(gap) * dt_ref[h : h + 1, :]).astype(BF)
            inner.append(jnp.dot(mix, xp, preferred_element_type=F32))
        carried = jnp.dot(
            c_map, ent_ref[at // width, :, at % width : at % width + 2 * head_dim],
            preferred_element_type=F32,
        )
        xf = xp.astype(F32)
        y = (
            jnp.where(lane < head_dim, inner[0], inner[1])
            + pair_lanes(rise[:, 2 * p : 2 * p + 1], rise[:, 2 * p + 1 : 2 * p + 2], rows, head_dim)
            * carried
            + skip_ref[:, span] * xf
        )
        u = y * silu(z_ref[:, span].astype(F32))
        u_ref[:, span] = u
        square = square + u * u
    scale = lax.rsqrt(jnp.sum(square, axis=1, keepdims=True) * (1.0 / cols) + 1e-5)
    out_ref[...] = (u_ref[...] * scale * gain_ref[...]).astype(BF)


def mixer(groups, xc, bc, cum, cum_t, dt, ent, gates, skip, gain):
    rows, xcols = xc.shape
    cols = xcols // groups
    mcols = bc.shape[1] // groups
    per_group = cum.shape[0] // groups
    parts = ent.shape[0] // groups
    return pl.pallas_call(
        mixer_kernel,
        out_shape=jax.ShapeDtypeStruct((rows, xcols), BF),
        grid=(groups,),
        in_specs=[
            pl.BlockSpec((rows, cols), lambda g: (0, g)),
            pl.BlockSpec((rows, mcols), lambda g: (0, g)),
            pl.BlockSpec((per_group, rows), lambda g: (g, 0)),
            pl.BlockSpec((1, rows, per_group), lambda g: (g, 0, 0)),
            pl.BlockSpec((per_group, rows), lambda g: (g, 0)),
            pl.BlockSpec((parts,) + ent.shape[1:], lambda g: (g, 0, 0)),
            pl.BlockSpec((rows, cols), lambda g: (0, g)),
            pl.BlockSpec((1, cols), lambda g: (0, g)),
            pl.BlockSpec((1, cols), lambda g: (0, g)),
        ],
        out_specs=pl.BlockSpec((rows, cols), lambda g: (0, g)),
        scratch_shapes=[pltpu.VMEM((rows, cols), F32)],
        compiler_params=pltpu.CompilerParams(vmem_limit_bytes=40 * 2**20),
        cost_estimate=pl.CostEstimate(
            flops=2 * rows * rows * xcols * 2, bytes_accessed=6 * rows * xcols,
            transcendentals=cum.shape[0] * rows * rows,
        ),
        name="mixer",
    )(xc, bc, cum, cum_t, dt, ent, gates, skip, gain)


def attend_kernel(together, q_ref, k_ref, v_ref, o_ref, peak_ref, acc_ref):
    c = lax.axis_index("ctx")
    rows = q_ref.shape[0]
    wide = min(4, k_ref.shape[0])
    keys = wide * rows
    tall = together * rows
    q = jnp.concatenate(
        [q_ref[:, i * HEAD_SIZE : (i + 1) * HEAD_SIZE] for i in range(together)], axis=0
    )
    scale = HEAD_SIZE**-0.5 * LOG2E

    def score(j):
        k = k_ref[pl.ds(j * wide, wide)].reshape(keys, HEAD_SIZE)
        return lax.dot_general(
            q, k, (((1,), (1,)), ((), ())), preferred_element_type=F32
        ) * scale

    def weigh(s, peak, v):
        w = jnp.exp2(s - peak).astype(BF)
        both = jnp.concatenate([v, jnp.ones((keys, HEAD_SIZE), BF)], axis=1)
        return jnp.dot(w, both, preferred_element_type=F32)

    top = lax.div(c, wide)
    tok = lax.rem(lax.broadcasted_iota(jnp.int32, (tall, keys), 0), rows) + lax.rem(c, wide) * rows
    pos = lax.broadcasted_iota(jnp.int32, (tall, keys), 1)
    s = jnp.where(pos <= tok, score(top), -1e30)
    peak = jnp.max(s, axis=1, keepdims=True)
    v = v_ref[pl.ds(top * wide, wide)].reshape(keys, HEAD_SIZE)
    held = lax.broadcasted_iota(jnp.int32, (keys, HEAD_SIZE), 0) < (lax.rem(c, wide) + 1) * rows
    acc_ref[...] = weigh(s, peak, jnp.where(held, v, jnp.zeros_like(v)))
    peak_ref[...] = jnp.broadcast_to(peak, peak_ref.shape)

    @pl.loop(0, top)
    def _(j):
        s = score(j)
        old = peak_ref[:, 0:1]
        peak = jnp.maximum(old, jnp.max(s, axis=1, keepdims=True))
        v = v_ref[pl.ds(j * wide, wide)].reshape(keys, HEAD_SIZE)
        acc_ref[...] = acc_ref[...] * jnp.exp2(old - peak) + weigh(s, peak, v)
        peak_ref[...] = jnp.broadcast_to(peak, peak_ref.shape)

    out = (acc_ref[:, :HEAD_SIZE] / acc_ref[:, HEAD_SIZE:]).astype(BF)
    for i in range(together):
        o_ref[:, i * HEAD_SIZE : (i + 1) * HEAD_SIZE] = out[i * rows : (i + 1) * rows]


def attend(queries, keys, values):
    rows, qcols = queries.shape
    n = keys.shape[0]
    together = 2
    steps = qcols // HEAD_SIZE // together
    per_kv = SHARED // together
    return pl.pallas_call(
        functools.partial(attend_kernel, together),
        out_shape=jax.ShapeDtypeStruct(queries.shape, BF),
        grid=(steps,),
        in_specs=[
            pl.BlockSpec((rows, together * HEAD_SIZE), lambda i: (0, i)),
            pl.BlockSpec((n, rows, HEAD_SIZE), lambda i: (0, 0, i // per_kv)),
            pl.BlockSpec((n, rows, HEAD_SIZE), lambda i: (0, 0, i // per_kv)),
        ],
        out_specs=pl.BlockSpec((rows, together * HEAD_SIZE), lambda i: (0, i)),
        scratch_shapes=[
            pltpu.VMEM((together * rows, 128), F32),
            pltpu.VMEM((together * rows, 2 * HEAD_SIZE), F32),
        ],
        compiler_params=pltpu.CompilerParams(vmem_limit_bytes=48 * 2**20),
        cost_estimate=pl.CostEstimate(
            flops=4 * n * rows * rows * qcols, bytes_accessed=4 * rows * qcols,
            transcendentals=n * rows * rows * qcols // HEAD_SIZE,
        ),
        name="attend",
    )(queries, keys, values)


def project_kernel(
    ways, chunks, a_ref, w_ref, o_ref,
    wbuf, lhs, mine, out1, in1, out2, in2,
    w_sem, send1, recv1, send2, recv2,
):
    tp = 2 * ways
    me = lax.axis_index("tp")
    core = lax.rem(me, 2)
    place = lax.div(me, 2)
    partner = place * 2 + 1 - core
    share = o_ref.shape[0]
    half = ways * share
    width = wbuf.shape[2]

    def w_copy(j):
        cols = pl.ds(pl.multiple_of(j * width, width), width)
        return pltpu.make_async_copy(w_ref.at[:, cols], wbuf.at[j], w_sem.at[j])

    for j in range(chunks):
        w_copy(j).start()

    barrier = pltpu.get_barrier_semaphore()
    for away in range(1, tp):
        pl.semaphore_signal(
            barrier, inc=1, device_id={"tp": lax.rem(me + away, tp)}, device_id_type=MESH
        )
    for x in range(ways):
        theirs = pl.multiple_of((2 * x + 1 - core) * share, share)
        ours = pl.multiple_of((2 * x + core) * share, share)
        lhs[x * share : (x + 1) * share] = a_ref[pl.ds(theirs, share)]
        lhs[half + x * share : half + (x + 1) * share] = a_ref[pl.ds(ours, share)]
    pl.semaphore_wait(barrier, tp - 1)

    def copy1(j):
        return pltpu.make_async_remote_copy(
            src_ref=out1.at[j], dst_ref=in1.at[j], send_sem=send1.at[j], recv_sem=recv1.at[j],
            device_id={"tp": partner}, device_id_type=MESH,
        )

    def copy2(j, away):
        other = lax.rem(place + away, ways)
        return pltpu.make_async_remote_copy(
            src_ref=out2.at[j, other], dst_ref=in2.at[j, ways - away],
            send_sem=send2.at[j, away], recv_sem=recv2.at[j, ways - away],
            device_id={"tp": other * 2 + core}, device_id_type=MESH,
        )

    def arrival2(j, away):
        other = lax.rem(place + away, ways)
        return pltpu.make_async_remote_copy(
            src_ref=out2.at[j, other], dst_ref=in2.at[j, away],
            send_sem=send2.at[j, away], recv_sem=recv2.at[j, away],
            device_id={"tp": other * 2 + core}, device_id_type=MESH,
        )

    def multiply(j):
        w_copy(j).wait()
        part = jnp.dot(lhs[...], wbuf[j], preferred_element_type=F32).astype(BF)
        out1[j] = part[:half]
        mine[j] = part[half:]
        copy1(j).start()

    def across(j):
        copy1(j).wait_recv()
        total = mine[j].astype(F32) + in1[j].astype(F32)
        for x in range(ways):
            out2[j, x] = total[x * share : (x + 1) * share].astype(BF)
        for away in range(1, ways):
            copy2(j, away).start()

    def finish(j):
        here = pl.ds(pl.multiple_of(place * share, share), share)
        total = mine[j, here].astype(F32) + in1[j, here].astype(F32)
        for away in range(1, ways):
            arrival2(j, away).wait_recv()
            total = total + in2[j, away].astype(F32)
        o_ref[:, pl.ds(pl.multiple_of(j * width, width), width)] = total.astype(BF)

    @pl.loop(0, chunks)
    def _(j):
        multiply(j)

        @pl.when(j >= 1)
        def _():
            across(j - 1)

    across(chunks - 1)

    @pl.loop(0, chunks)
    def _(j):
        finish(j)

    for j in range(chunks):
        copy1(j).wait_send()
        for away in range(1, ways):
            copy2(j, away).wait_send()


def project(tp, normed, weight):
    rows, depth = normed.shape
    cols = weight.shape[1]
    width = 512
    chunks = cols // width
    ways = tp // 2
    share = rows // tp
    half = ways * share
    vm = pl.BlockSpec(memory_space=pltpu.VMEM)
    dma = pltpu.SemaphoreType.DMA
    return pl.pallas_call(
        functools.partial(project_kernel, ways, chunks),
        out_shape=jax.ShapeDtypeStruct((share, cols), BF),
        in_specs=[vm, pl.BlockSpec(memory_space=pl.ANY)],
        out_specs=vm,
        scratch_shapes=[
            pltpu.VMEM((chunks, depth, width), BF),
            pltpu.VMEM((rows, depth), BF),
            pltpu.VMEM((chunks, half, width), BF),
            pltpu.VMEM((chunks, half, width), BF),
            pltpu.VMEM((chunks, half, width), BF),
            pltpu.VMEM((chunks, ways, share, width), BF),
            pltpu.VMEM((chunks, ways, share, width), BF),
            dma((chunks,)), dma((chunks,)), dma((chunks,)),
            dma((chunks, ways)), dma((chunks, ways)),
        ],
        compiler_params=pltpu.CompilerParams(
            collective_id=1, has_side_effects=True, vmem_limit_bytes=48 * 2**20
        ),
        name="project",
    )(normed, weight)


def per_device(
    n, tp, ssm_inputs, state_maps, ssm_gates, time_steps, log_rates, skip_gain, conv_inputs, conv_maps,
    norm_gain, out_weight, queries, attention_keys, values,
):
    rows, xcols = ssm_inputs.shape
    groups = state_maps.shape[1]
    heads = log_rates.shape[0]
    xc, bc, cum, cum_t, dt, ent, kbuf, vbuf = exchange(
        n, groups, ssm_inputs, state_maps.reshape(rows, -1), time_steps,
        log_rates.reshape(heads, 1), conv_inputs, conv_maps.reshape(conv_maps.shape[0], -1),
        attention_keys, values,
    )
    skip = jnp.repeat(skip_gain, xcols // heads).reshape(1, xcols)
    normed = mixer(
        groups, xc, bc, cum, cum_t, dt, ent.reshape((-1,) + ent.shape[2:]), ssm_gates, skip,
        norm_gain.reshape(1, xcols),
    )
    ssm_out = project(tp, normed, out_weight)
    attn_out = attend(queries, kbuf, vbuf)
    return (ssm_out, attn_out)


def solution(mesh):
    placed = (
        P("ctx", "tp"),
        P("ctx", "tp", None),
        P("ctx", "tp"),
        P("tp", "ctx"),
        P("tp"),
        P("tp"),
        P(None, "tp"),
        P(None, "tp", None),
        P("tp"),
        P("tp", None),
        P("ctx", "tp"),
        P("ctx", "tp"),
        P("ctx", "tp"),
    )
    return jax.shard_map(
        functools.partial(per_device, mesh.shape["ctx"], mesh.shape["tp"]),
        mesh=mesh,
        in_specs=placed,
        out_specs=(P(("ctx", "tp"), None), P("ctx", "tp")),
        check_vma=False,
    )
```

```python
import functools

import jax
import jax.numpy as jnp
from jax import lax
from jax.experimental import pallas as pl
from jax.experimental.pallas import tpu as pltpu
from jax.sharding import PartitionSpec as P

HEAD_SIZE = 128
SHARED = 8
MESH = pl.DeviceIdType.MESH
LOG2E = 1.4426950408889634
BF = jnp.bfloat16
F32 = jnp.float32


def pair_lanes(col_a, col_b, rows, head_dim):
    lane = lax.broadcasted_iota(jnp.int32, (rows, 2 * head_dim), 1)
    return jnp.where(
        lane < head_dim,
        jnp.broadcast_to(col_a, (rows, 2 * head_dim)),
        jnp.broadcast_to(col_b, (rows, 2 * head_dim)),
    )


def silu(v):
    return v / (1.0 + jnp.exp(-v))


def mix_group(g, groups, xc_ref, bc_ref, cum_ref, cumt_ref, dt_ref, ent_ref, z_ref, skip_ref, gain_ref,
              out_ref, u_ref):
    rows = xc_ref.shape[0]
    cols = xc_ref.shape[1] // groups
    per_group = cum_ref.shape[0] // groups
    head_dim = cols // per_group
    nstate = bc_ref.shape[1] // groups // 2
    chunks, width = ent_ref.shape[1], ent_ref.shape[3]
    part = chunks * width
    b_map = bc_ref[:, 2 * g * nstate : (2 * g + 1) * nstate]
    c_map = bc_ref[:, (2 * g + 1) * nstate : (2 * g + 2) * nstate]
    products = lax.dot_general(
        c_map, b_map, (((1,), (1,)), ((), ())), preferred_element_type=F32
    )
    tok = lax.broadcasted_iota(jnp.int32, (rows, rows), 0)
    src = lax.broadcasted_iota(jnp.int32, (rows, rows), 1)
    products = jnp.where(tok >= src, products, 0.0)
    cum_t = cumt_ref[g]
    rise = jnp.exp(cum_t)
    square = jnp.zeros((rows, 2 * head_dim), F32)
    lane = lax.broadcasted_iota(jnp.int32, (rows, 2 * head_dim), 1)
    for p in range(per_group // 2):
        at = g * cols + 2 * p * head_dim
        span = slice(at, at + 2 * head_dim)
        local = slice(2 * p * head_dim, 2 * (p + 1) * head_dim)
        xp = xc_ref[:, span]
        inner = []
        for h in (2 * p, 2 * p + 1):
            row = slice(g * per_group + h, g * per_group + h + 1)
            gap = jnp.minimum(cum_t[:, h : h + 1] - cum_ref[row, :], 0.0)
            mix = (products * jnp.exp(gap) * dt_ref[row, :]).astype(BF)
            inner.append(jnp.dot(mix, xp, preferred_element_type=F32))
        inside = at % width
        carried = jnp.dot(
            c_map, ent_ref[at // part, (at % part) // width, :, inside : inside + 2 * head_dim],
            preferred_element_type=F32,
        )
        xf = xp.astype(F32)
        h = g * per_group + 2 * p
        y = (
            jnp.where(lane < head_dim, inner[0], inner[1])
            + pair_lanes(rise[:, 2 * p : 2 * p + 1], rise[:, 2 * p + 1 : 2 * p + 2], rows, head_dim)
            * carried
            + pair_lanes(skip_ref[0:1, h : h + 1], skip_ref[0:1, h + 1 : h + 2], 1, head_dim) * xf
        )
        u = y * silu(z_ref[:, span].astype(F32))
        u_ref[:, local] = u
        square = square + u * u
    scale = lax.rsqrt(jnp.sum(square, axis=1, keepdims=True) * (1.0 / cols) + 1e-5)
    own = slice(g * cols, (g + 1) * cols)
    out_ref[:, own] = (u_ref[...] * scale * gain_ref[0:1, own]).astype(BF)


def attend_step(i, c, q_ref, k_ref, v_ref, o_ref, peak_ref, acc_ref):
    rows = q_ref.shape[0]
    wide = min(4, k_ref.shape[0])
    keys = wide * rows
    together = acc_ref.shape[0]
    per_kv = SHARED // together
    span = together * HEAD_SIZE
    head = pl.ds(pl.multiple_of(lax.div(i, per_kv) * HEAD_SIZE, HEAD_SIZE), HEAD_SIZE)
    here = pl.ds(pl.multiple_of(i * span, span), span)
    q_all = q_ref[:, here]
    qs = [q_all[:, t * HEAD_SIZE : (t + 1) * HEAD_SIZE] for t in range(together)]
    scale = HEAD_SIZE**-0.5 * LOG2E

    def scores(j):
        k = k_ref[pl.ds(j * wide, wide), :, head].reshape(keys, HEAD_SIZE)
        return [
            lax.dot_general(q, k, (((1,), (1,)), ((), ())), preferred_element_type=F32) * scale
            for q in qs
        ]

    def weigh(s, peak, both):
        return jnp.dot(jnp.exp2(s - peak).astype(BF), both, preferred_element_type=F32)

    def widened(v):
        return jnp.concatenate([v, jnp.ones((keys, HEAD_SIZE), BF)], axis=1)

    top = lax.div(c, wide)
    offset = lax.rem(c, wide) * rows
    tok = lax.broadcasted_iota(jnp.int32, (rows, keys), 0) + offset
    pos = lax.broadcasted_iota(jnp.int32, (rows, keys), 1)
    allowed = pos <= tok
    v = v_ref[pl.ds(top * wide, wide), :, head].reshape(keys, HEAD_SIZE)
    held = lax.broadcasted_iota(jnp.int32, (keys, HEAD_SIZE), 0) < offset + rows
    both = widened(jnp.where(held, v, jnp.zeros_like(v)))
    for t, s in enumerate(scores(top)):
        s = jnp.where(allowed, s, -1e30)
        peak = jnp.max(s, axis=1, keepdims=True)
        acc_ref[t] = weigh(s, peak, both)
        peak_ref[t] = jnp.broadcast_to(peak, peak_ref.shape[1:])

    @pl.loop(0, top)
    def _(j):
        v = v_ref[pl.ds(j * wide, wide), :, head].reshape(keys, HEAD_SIZE)
        both = widened(v)
        for t, s in enumerate(scores(j)):
            old = peak_ref[t][:, 0:1]
            peak = jnp.maximum(old, jnp.max(s, axis=1, keepdims=True))
            acc_ref[t] = acc_ref[t] * jnp.exp2(old - peak) + weigh(s, peak, both)
            peak_ref[t] = jnp.broadcast_to(peak, peak_ref.shape[1:])

    o_ref[:, here] = jnp.concatenate(
        [(acc_ref[t][:, :HEAD_SIZE] / acc_ref[t][:, HEAD_SIZE:]).astype(BF) for t in range(together)],
        axis=1,
    )


def layer_kernel(
    n, inner, chunks, groups, ways, steps_out,
    x_in, maps_in, z_in, steps_in, rates_in, skip_in, tapx_in, tapm_in, gain_in, w_ref, q_in, k_ref, v_ref,
    o_ref, attn_ref,
    x_ref, maps_ref, z_ref, steps_ref, rates_ref, skip_ref, tapx_ref, tapm_ref, gain_ref, q_ref, in_sem,
    xc_ref, bc_ref, cum_ref, cumt_ref, dt_ref, ent_ref, kbuf, vbuf,
    halo_x, halo_m, ext, wbuf, srow, rrow, ein, eout, pbuf,
    halo_send, halo_recv, own_sem, kz_send, vz_send, kr_send, vr_send, k_recv, v_recv,
    s_send, s_recv, e_send, e_recv, p_send, p_recv,
    u_ref, nbuf, peak_ref, acc_ref,
    w_buf, lhs, mine, out1, in1, out2, in2,
    w_sem, send1, recv1, send2, recv2,
):
    outer = n // inner
    c = lax.axis_index("ctx")
    hi = lax.div(c, inner)
    lo = lax.rem(c, inner)
    rows, xcols = x_ref.shape
    mcols = maps_ref.shape[1]
    heads = steps_ref.shape[0]
    head_dim = xcols // heads
    nstate = mcols // groups // 2
    width = srow.shape[3]
    part = width * chunks

    def remote(src, dst, send, recv, place):
        return pltpu.make_async_remote_copy(
            src_ref=src, dst_ref=dst, send_sem=send, recv_sem=recv,
            device_id={"ctx": place}, device_id_type=MESH,
        )

    inputs = [
        pltpu.make_async_copy(src, dst, in_sem.at[i])
        for i, (src, dst) in enumerate((
            (x_in, x_ref), (maps_in, maps_ref), (steps_in, steps_ref), (rates_in, rates_ref),
            (tapx_in, tapx_ref), (tapm_in, tapm_ref), (skip_in, skip_ref), (gain_in, gain_ref),
            (q_in, q_ref), (z_in, z_ref),
        ))
    ]
    for copy in inputs:
        copy.start()

    tp = 2 * ways
    me = lax.axis_index("tp")
    core = lax.rem(me, 2)
    place = lax.div(me, 2)
    partner = place * 2 + 1 - core
    share = o_ref.shape[0]
    half = ways * share
    out_width = w_buf.shape[2]

    def w_copy(j):
        cols = pl.ds(pl.multiple_of(j * out_width, out_width), out_width)
        return pltpu.make_async_copy(w_ref.at[:, cols], w_buf.at[j], w_sem.at[j])

    barrier = pltpu.get_barrier_semaphore()
    for away in range(1, tp):
        pl.semaphore_signal(
            barrier, inc=1, device_id={"tp": lax.rem(me + away, tp)}, device_id_type=MESH
        )
    for away in range(1, n):
        pl.semaphore_signal(
            barrier, inc=1, device_id={"ctx": lax.rem(c + away, n)}, device_id_type=MESH
        )
    for copy in inputs[:2]:
        copy.wait()
    pl.semaphore_wait(barrier, n + tp - 2)

    up = lax.rem(c + inner, n)
    nxt = lax.rem(c + 1, n)

    def kv_up(src_k, src_v, block):
        return (
            remote(src_k, kbuf.at[block], kz_send.at[block], k_recv.at[block], up),
            remote(src_v, vbuf.at[block], vz_send.at[block], v_recv.at[block], up),
        )

    def kv_row(src_k, src_v, block, peer):
        place = hi * inner + peer
        return (
            remote(src_k, kbuf.at[block], kr_send.at[block, peer], k_recv.at[block], place),
            remote(src_v, vbuf.at[block], vr_send.at[block, peer], v_recv.at[block], place),
        )

    def halo_copies():
        return (
            remote(x_ref.at[pl.ds(rows - 16, 16)], halo_x, halo_send.at[0], halo_recv.at[0], nxt),
            remote(maps_ref.at[pl.ds(rows - 16, 16)], halo_m, halo_send.at[1], halo_recv.at[1], nxt),
        )

    @pl.when(c < n - 1)
    def _():
        for copy in halo_copies():
            copy.start()

    @pl.when(hi < outer - 1)
    def _():
        for copy in kv_up(k_ref, v_ref, c):
            copy.start()

    for away in range(1, inner):
        peer = lax.rem(lo + away, inner)

        @pl.when(peer > lo)
        def _():
            for copy in kv_row(k_ref, v_ref, c, peer):
                copy.start()

    own = (
        pltpu.make_async_copy(k_ref, kbuf.at[c], own_sem.at[0]),
        pltpu.make_async_copy(v_ref, vbuf.at[c], own_sem.at[1]),
    )
    for copy in own:
        copy.start()

    for j in range(steps_out):
        w_copy(j).start()
    for copy in inputs[2:]:
        copy.wait()

    raw = steps_ref[...]
    dt = jnp.maximum(raw, 0.0) + jnp.log1p(jnp.exp(-jnp.abs(raw)))
    square = (heads, heads)
    rates = jnp.sum(
        jnp.where(
            lax.broadcasted_iota(jnp.int32, square, 0) == lax.broadcasted_iota(jnp.int32, square, 1),
            jnp.broadcast_to(rates_ref[...], square), 0.0,
        ),
        axis=1, keepdims=True,
    )
    cum = dt * -jnp.exp(rates)
    lane = lax.broadcasted_iota(jnp.int32, cum.shape, 1)
    reach = 1
    while reach < rows:
        cum = cum + jnp.where(lane >= reach, pltpu.roll(cum, reach, 1), 0.0)
        reach *= 2
    cum_ref[...] = cum
    dt_ref[...] = dt
    per_group = heads // groups
    last = cum[:, rows - 1 : rows]
    tail = (jnp.exp(last - cum) * dt).T
    cum_t = cum.T
    for g in range(groups):
        cumt_ref[g] = cum_t[:, g * per_group : (g + 1) * per_group]
    end_decay = jnp.exp(cum_t[rows - 1 : rows])

    @pl.when(c == 0)
    def _():
        halo_x[...] = jnp.zeros_like(halo_x)
        halo_m[...] = jnp.zeros_like(halo_m)

    @pl.when(c > 0)
    def _():
        for copy in halo_copies():
            copy.wait_recv()

    taps = tapx_ref.shape[0]
    step = 256

    def conv(src, halo, tap_ref, dst, cols):
        ext[0:8, :] = halo[:, cols].astype(F32)[8:16]
        ext[8 : 8 + rows, :] = src[:, cols].astype(F32)
        tap = tap_ref[:, cols].astype(F32)
        total = jnp.zeros((rows, step), F32)
        for k in range(taps):
            total = total + tap[k : k + 1] * ext[pl.ds(9 - taps + k, rows), :]
        dst[:, cols] = silu(total).astype(BF)

    for j in range(mcols // step):
        conv(maps_ref, halo_m, tapm_ref, bc_ref, slice(j * step, (j + 1) * step))
    for j in range(xcols // step):
        conv(x_ref, halo_x, tapx_ref, xc_ref, slice(j * step, (j + 1) * step))

    for p in range(heads // 2):
        cols = slice(2 * p * head_dim, 2 * (p + 1) * head_dim)
        weight = pair_lanes(
            tail[:, 2 * p : 2 * p + 1], tail[:, 2 * p + 1 : 2 * p + 2], rows, head_dim
        )
        wbuf[:, cols] = (weight * xc_ref[:, cols].astype(F32)).astype(BF)
        at = 2 * p * head_dim
        srow[at // part, (at % part) // width, nstate : nstate + 16,
             at % width : at % width + 2 * head_dim] = pair_lanes(
            end_decay[:, 2 * p : 2 * p + 1], end_decay[:, 2 * p + 1 : 2 * p + 2], 16, head_dim
        ).astype(BF)
    group_cols = xcols // groups
    for m in range(inner):
        for ch in range(chunks):
            at = m * part + ch * width
            g = at // group_cols
            b_map = bc_ref[:, g * 2 * nstate : g * 2 * nstate + nstate]
            srow[m, ch, 0:nstate] = lax.dot_general(
                b_map, wbuf[:, at : at + width], (((0,), (0,)), ((), ())),
                preferred_element_type=F32,
            ).astype(BF)

    def s_copy(peer, ch):
        return remote(
            srow.at[peer, ch], rrow.at[lo, ch], s_send.at[peer, ch], s_recv.at[lo, ch],
            hi * inner + peer,
        )

    def s_arrival(peer, ch):
        return remote(
            srow.at[peer, ch], rrow.at[peer, ch], s_send.at[peer, ch], s_recv.at[peer, ch],
            hi * inner + peer,
        )

    for ch in range(chunks):
        for away in range(1, inner):
            s_copy(lax.rem(lo + away, inner), ch).start()
        rrow[lo, ch] = srow[lo, ch]

    for k in range(1, outer):
        block = lax.rem(c - k * inner + n, n)

        @pl.when(hi >= k)
        def _():
            for copy in kv_up(kbuf.at[block], vbuf.at[block], block):
                copy.wait_recv()

            @pl.when(hi < outer - 1)
            def _():
                for copy in kv_up(kbuf.at[block], vbuf.at[block], block):
                    copy.start()

            for away in range(1, inner):
                for copy in kv_row(kbuf.at[block], vbuf.at[block], block, lax.rem(lo + away, inner)):
                    copy.start()

    for copy in own:
        copy.wait()
    for k in range(outer):
        for away in range(1, inner):
            peer = lax.rem(lo + away, inner)
            theirs = lax.rem(hi - k + outer, outer) * inner + peer

            @pl.when((hi >= k) if k else (peer < lo))
            def _():
                for copy in kv_row(kbuf.at[theirs], vbuf.at[theirs], theirs, peer):
                    copy.wait_recv()

    steps_attn = q_ref.shape[1] // HEAD_SIZE // acc_ref.shape[0]
    early = jnp.minimum(steps_attn // 2, 2 * jnp.maximum(hi - 1, 0))

    @pl.loop(0, early)
    def _(i):
        attend_step(i, c, q_ref, kbuf, vbuf, attn_ref, peak_ref, acc_ref)

    def e_copy(ch):
        return remote(eout.at[ch], ein.at[ch], e_send.at[ch], e_recv.at[ch], up)

    def p_copy(peer, ch):
        return remote(
            pbuf.at[peer, ch], ent_ref.at[lo, ch], p_send.at[peer, ch], p_recv.at[lo, ch],
            hi * inner + peer,
        )

    def p_arrival(peer, ch):
        return remote(
            pbuf.at[peer, ch], ent_ref.at[peer, ch], p_send.at[peer, ch], p_recv.at[peer, ch],
            hi * inner + peer,
        )

    for ch in range(chunks):
        for away in range(1, inner):
            s_arrival(lax.rem(lo + away, inner), ch).wait_recv()

        @pl.when(hi == 0)
        def _():
            ein[ch] = jnp.zeros_like(ein[ch])

        @pl.when(hi > 0)
        def _():
            e_copy(ch).wait_recv()

        state = ein[ch].astype(F32)
        for m in range(inner):
            pbuf[m, ch] = state.astype(BF)
            state = rrow[m, ch, nstate : nstate + 16].astype(F32)[0:1] * state + rrow[
                m, ch, 0:nstate
            ].astype(F32)
        eout[ch] = state.astype(BF)

        @pl.when(hi < outer - 1)
        def _():
            e_copy(ch).start()

        for away in range(1, inner):
            p_copy(lax.rem(lo + away, inner), ch).start()
        ent_ref[lo, ch] = pbuf[lo, ch]

    for ch in range(chunks):
        for away in range(1, inner):
            p_arrival(lax.rem(lo + away, inner), ch).wait_recv()

    for g in range(groups):
        mix_group(g, groups, xc_ref, bc_ref, cum_ref, cumt_ref, dt_ref, ent_ref, z_ref, skip_ref,
                  gain_ref, nbuf, u_ref)

    for x in range(ways):
        theirs = pl.multiple_of((2 * x + 1 - core) * share, share)
        ours = pl.multiple_of((2 * x + core) * share, share)
        lhs[x * share : (x + 1) * share] = nbuf[pl.ds(theirs, share)]
        lhs[half + x * share : half + (x + 1) * share] = nbuf[pl.ds(ours, share)]

    def copy1(j):
        return pltpu.make_async_remote_copy(
            src_ref=out1.at[j], dst_ref=in1.at[j], send_sem=send1.at[j], recv_sem=recv1.at[j],
            device_id={"tp": partner}, device_id_type=MESH,
        )

    def copy2(j, away):
        other = lax.rem(place + away, ways)
        return pltpu.make_async_remote_copy(
            src_ref=out2.at[j, other], dst_ref=in2.at[j, ways - away],
            send_sem=send2.at[j, away], recv_sem=recv2.at[j, ways - away],
            device_id={"tp": other * 2 + core}, device_id_type=MESH,
        )

    def arrival2(j, away):
        other = lax.rem(place + away, ways)
        return pltpu.make_async_remote_copy(
            src_ref=out2.at[j, other], dst_ref=in2.at[j, away],
            send_sem=send2.at[j, away], recv_sem=recv2.at[j, away],
            device_id={"tp": other * 2 + core}, device_id_type=MESH,
        )

    def multiply(j):
        w_copy(j).wait()
        part = jnp.dot(lhs[...], w_buf[j], preferred_element_type=F32).astype(BF)
        out1[j] = part[:half]
        mine[j] = part[half:]
        copy1(j).start()

    def across(j):
        copy1(j).wait_recv()
        total = mine[j].astype(F32) + in1[j].astype(F32)
        for x in range(ways):
            out2[j, x] = total[x * share : (x + 1) * share].astype(BF)
        for away in range(1, ways):
            copy2(j, away).start()

    def finish(j):
        here = pl.ds(pl.multiple_of(place * share, share), share)
        total = mine[j, here].astype(F32) + in1[j, here].astype(F32)
        for away in range(1, ways):
            arrival2(j, away).wait_recv()
            total = total + in2[j, away].astype(F32)
        o_ref[:, pl.ds(pl.multiple_of(j * out_width, out_width), out_width)] = total.astype(BF)

    @pl.loop(0, steps_out)
    def _(j):
        multiply(j)

        @pl.when(j >= 1)
        def _():
            across(j - 1)

    across(steps_out - 1)

    @pl.loop(early, steps_attn)
    def _(i):
        attend_step(i, c, q_ref, kbuf, vbuf, attn_ref, peak_ref, acc_ref)

    @pl.loop(0, steps_out)
    def _(j):
        finish(j)

    for j in range(steps_out):
        copy1(j).wait_send()
        for away in range(1, ways):
            copy2(j, away).wait_send()

    for k in range(outer):
        block = lax.rem(c - k * inner + n, n)
        for away in range(1, inner):
            peer = lax.rem(lo + away, inner)

            @pl.when((hi >= k) if k else (peer > lo))
            def _():
                for copy in kv_row(kbuf.at[block], vbuf.at[block], block, peer):
                    copy.wait_send()

        @pl.when((hi >= k) & (hi < outer - 1))
        def _():
            for copy in kv_up(kbuf.at[block], vbuf.at[block], block):
                copy.wait_send()

    for ch in range(chunks):
        for away in range(1, inner):
            peer = lax.rem(lo + away, inner)
            s_copy(peer, ch).wait_send()
            p_copy(peer, ch).wait_send()

        @pl.when(hi < outer - 1)
        def _():
            e_copy(ch).wait_send()

    @pl.when(c < n - 1)
    def _():
        for copy in halo_copies():
            copy.wait_send()


def per_device(
    n, tp, ssm_inputs, state_maps, ssm_gates, time_steps, log_rates, skip_gain, conv_inputs, conv_maps,
    norm_gain, out_weight, queries, attention_keys, values,
):
    rows, xcols = ssm_inputs.shape
    groups = state_maps.shape[1]
    heads = log_rates.shape[0]
    maps = state_maps.reshape(rows, -1)
    mcols = maps.shape[1]
    taps = conv_inputs.shape[0]
    nstate = mcols // groups // 2
    depth, cols = out_weight.shape
    inner = 2 if n <= 8 else 8
    part = xcols // inner
    chunks = max(1, part // 512)
    width = part // chunks
    ways = tp // 2
    share = rows // tp
    half = ways * share
    out_width = 512
    steps = cols // out_width
    kvcols = attention_keys.shape[1]
    vm = pl.BlockSpec(memory_space=pltpu.VMEM)
    hbm = pl.BlockSpec(memory_space=pl.ANY)
    dma = pltpu.SemaphoreType.DMA
    return pl.pallas_call(
        functools.partial(layer_kernel, n, inner, chunks, groups, ways, steps),
        out_shape=(
            jax.ShapeDtypeStruct((share, cols), BF),
            jax.ShapeDtypeStruct(queries.shape, BF),
        ),
        in_specs=[hbm] * 13,
        out_specs=(vm, vm),
        scratch_shapes=[
            pltpu.VMEM((rows, xcols), BF),
            pltpu.VMEM((rows, mcols), BF),
            pltpu.VMEM((rows, xcols), BF),
            pltpu.VMEM((heads, rows), F32),
            pltpu.VMEM((1, heads), F32),
            pltpu.VMEM((1, heads), F32),
            pltpu.VMEM((taps, xcols), BF),
            pltpu.VMEM((taps, mcols), BF),
            pltpu.VMEM((1, xcols), F32),
            pltpu.VMEM(queries.shape, BF),
            dma((10,)),
            pltpu.VMEM((rows, xcols), BF),
            pltpu.VMEM((rows, mcols), BF),
            pltpu.VMEM((heads, rows), F32),
            pltpu.VMEM((groups, rows, heads // groups), F32),
            pltpu.VMEM((heads, rows), F32),
            pltpu.VMEM((inner, chunks, nstate, width), BF),
            pltpu.VMEM((n, rows, kvcols), BF),
            pltpu.VMEM((n, rows, kvcols), BF),
            pltpu.VMEM((16, xcols), BF),
            pltpu.VMEM((16, mcols), BF),
            pltpu.VMEM((rows + 8, 256), F32),
            pltpu.VMEM((rows, xcols), BF),
            pltpu.VMEM((inner, chunks, nstate + 16, width), BF),
            pltpu.VMEM((inner, chunks, nstate + 16, width), BF),
            pltpu.VMEM((chunks, nstate, width), BF),
            pltpu.VMEM((chunks, nstate, width), BF),
            pltpu.VMEM((inner, chunks, nstate, width), BF),
            dma((2,)), dma((2,)), dma((2,)),
            dma((n,)), dma((n,)), dma((n, inner)), dma((n, inner)), dma((n,)), dma((n,)),
            dma((inner, chunks)), dma((inner, chunks)),
            dma((chunks,)), dma((chunks,)),
            dma((inner, chunks)), dma((inner, chunks)),
            pltpu.VMEM((rows, xcols // groups), F32),
            pltpu.VMEM((rows, xcols), BF),
            pltpu.VMEM((2, rows, 128), F32),
            pltpu.VMEM((2, rows, 2 * HEAD_SIZE), F32),
            pltpu.VMEM((steps, depth, out_width), BF),
            pltpu.VMEM((rows, depth), BF),
            pltpu.VMEM((steps, half, out_width), BF),
            pltpu.VMEM((steps, half, out_width), BF),
            pltpu.VMEM((steps, half, out_width), BF),
            pltpu.VMEM((steps, ways, share, out_width), BF),
            pltpu.VMEM((steps, ways, share, out_width), BF),
            dma((steps,)), dma((steps,)), dma((steps,)),
            dma((steps, ways)), dma((steps, ways)),
        ],
        compiler_params=pltpu.CompilerParams(
            collective_id=0, has_side_effects=True, vmem_limit_bytes=58 * 2**20
        ),
        name="layer",
    )(
        ssm_inputs, maps, ssm_gates, time_steps, log_rates.reshape(1, heads),
        skip_gain.reshape(1, heads), conv_inputs, conv_maps.reshape(taps, mcols),
        norm_gain.reshape(1, xcols), out_weight, queries, attention_keys, values,
    )


def solution(mesh):
    placed = (
        P("ctx", "tp"),
        P("ctx", "tp", None),
        P("ctx", "tp"),
        P("tp", "ctx"),
        P("tp"),
        P("tp"),
        P(None, "tp"),
        P(None, "tp", None),
        P("tp"),
        P("tp", None),
        P("ctx", "tp"),
        P("ctx", "tp"),
        P("ctx", "tp"),
    )
    return jax.shard_map(
        functools.partial(per_device, mesh.shape["ctx"], mesh.shape["tp"]),
        mesh=mesh,
        in_specs=placed,
        out_specs=(P(("ctx", "tp"), None), P("ctx", "tp")),
        check_vma=False,
    )
```

```python
import functools

import jax
import jax.numpy as jnp
from jax import lax
from jax.experimental import pallas as pl
from jax.experimental.pallas import tpu as pltpu
from jax.sharding import PartitionSpec as P

HEAD_SIZE = 128
SHARED = 8
MESH = pl.DeviceIdType.MESH
LOG2E = 1.4426950408889634
BF = jnp.bfloat16
F32 = jnp.float32


def pair_lanes(col_a, col_b, rows, head_dim):
    lane = lax.broadcasted_iota(jnp.int32, (rows, 2 * head_dim), 1)
    return jnp.where(
        lane < head_dim,
        jnp.broadcast_to(col_a, (rows, 2 * head_dim)),
        jnp.broadcast_to(col_b, (rows, 2 * head_dim)),
    )


def silu(v):
    return v / (1.0 + jnp.exp(-v))


def mix_inside(g, groups, xc_ref, bc_ref, cum_ref, cumt_ref, dt_ref, skip_ref, y_ref):
    rows = xc_ref.shape[0]
    cols = xc_ref.shape[1] // groups
    per_group = cum_ref.shape[0] // groups
    head_dim = cols // per_group
    nstate = bc_ref.shape[1] // groups // 2
    b_map = bc_ref[:, 2 * g * nstate : (2 * g + 1) * nstate]
    c_map = bc_ref[:, (2 * g + 1) * nstate : (2 * g + 2) * nstate]
    products = lax.dot_general(
        c_map, b_map, (((1,), (1,)), ((), ())), preferred_element_type=F32
    )
    tok = lax.broadcasted_iota(jnp.int32, (rows, rows), 0)
    src = lax.broadcasted_iota(jnp.int32, (rows, rows), 1)
    products = jnp.where(tok >= src, products, 0.0)
    cum_t = cumt_ref[g]
    lane = lax.broadcasted_iota(jnp.int32, (rows, 2 * head_dim), 1)
    for p in range(per_group // 2):
        at = g * cols + 2 * p * head_dim
        span = slice(at, at + 2 * head_dim)
        xp = xc_ref[:, span]
        inner = []
        for h in (2 * p, 2 * p + 1):
            row = slice(g * per_group + h, g * per_group + h + 1)
            gap = jnp.minimum(cum_t[:, h : h + 1] - cum_ref[row, :], 0.0)
            mix = (products * jnp.exp(gap) * dt_ref[row, :]).astype(BF)
            inner.append(jnp.dot(mix, xp, preferred_element_type=F32))
        h = g * per_group + 2 * p
        skip = pair_lanes(skip_ref[0:1, h : h + 1], skip_ref[0:1, h + 1 : h + 2], 1, head_dim)
        y_ref[:, span] = jnp.where(lane < head_dim, inner[0], inner[1]) + skip * xp.astype(F32)


def mix_finish(g, groups, bc_ref, cumt_ref, ent_ref, z_ref, gain_ref, out_ref, y_ref):
    rows = z_ref.shape[0]
    cols = z_ref.shape[1] // groups
    per_group = cumt_ref.shape[2]
    head_dim = cols // per_group
    nstate = bc_ref.shape[1] // groups // 2
    chunks, width = ent_ref.shape[1], ent_ref.shape[3]
    part = chunks * width
    c_map = bc_ref[:, (2 * g + 1) * nstate : (2 * g + 2) * nstate]
    rise = jnp.exp(cumt_ref[g])
    square = jnp.zeros((rows, 2 * head_dim), F32)
    for p in range(per_group // 2):
        at = g * cols + 2 * p * head_dim
        span = slice(at, at + 2 * head_dim)
        inside = at % width
        carried = jnp.dot(
            c_map, ent_ref[at // part, (at % part) // width, :, inside : inside + 2 * head_dim],
            preferred_element_type=F32,
        )
        y = y_ref[:, span] + carried * pair_lanes(
            rise[:, 2 * p : 2 * p + 1], rise[:, 2 * p + 1 : 2 * p + 2], rows, head_dim
        )
        u = y * silu(z_ref[:, span].astype(F32))
        y_ref[:, span] = u
        square = square + u * u
    scale = lax.rsqrt(jnp.sum(square, axis=1, keepdims=True) * (1.0 / cols) + 1e-5)
    own = slice(g * cols, (g + 1) * cols)
    out_ref[:, own] = (y_ref[:, own] * scale * gain_ref[0:1, own]).astype(BF)


def attend_step(i, c, q_ref, k_ref, v_ref, o_ref, peak_ref, acc_ref):
    rows = q_ref.shape[0]
    wide = min(4, k_ref.shape[0])
    keys = wide * rows
    chains, tall = acc_ref.shape[:2]
    together = chains * tall // rows
    per_chain = tall // rows
    per_kv = SHARED // together
    span = together * HEAD_SIZE
    head = pl.ds(pl.multiple_of(lax.div(i, per_kv) * HEAD_SIZE, HEAD_SIZE), HEAD_SIZE)
    here = pl.ds(pl.multiple_of(i * span, span), span)
    q_all = q_ref[:, here]
    qs = [
        jnp.concatenate(
            [q_all[:, h * HEAD_SIZE : (h + 1) * HEAD_SIZE]
             for h in range(t * per_chain, (t + 1) * per_chain)], axis=0
        )
        for t in range(chains)
    ]
    scale = HEAD_SIZE**-0.5 * LOG2E

    def scores(j):
        k = jnp.concatenate([k_ref[j * wide + b, head, :] for b in range(wide)], axis=1)
        return [jnp.dot(q, k, preferred_element_type=F32) * scale for q in qs]

    def weigh(s, peak, both):
        return jnp.dot(jnp.exp2(s - peak).astype(BF), both, preferred_element_type=F32)

    def widened(v):
        return jnp.concatenate([v, jnp.ones((keys, HEAD_SIZE), BF)], axis=1)

    top = lax.div(c, wide)
    offset = lax.rem(c, wide) * rows
    tok = lax.rem(lax.broadcasted_iota(jnp.int32, (tall, keys), 0), rows) + offset
    pos = lax.broadcasted_iota(jnp.int32, (tall, keys), 1)
    allowed = pos <= tok
    v = v_ref[pl.ds(top * wide, wide), :, head].reshape(keys, HEAD_SIZE)
    held = lax.broadcasted_iota(jnp.int32, (keys, HEAD_SIZE), 0) < offset + rows
    both = widened(jnp.where(held, v, jnp.zeros_like(v)))
    for t, s in enumerate(scores(top)):
        s = jnp.where(allowed, s, -1e30)
        peak = jnp.max(s, axis=1, keepdims=True)
        acc_ref[t] = weigh(s, peak, both)
        peak_ref[t] = jnp.broadcast_to(peak, peak_ref.shape[1:])

    @pl.loop(0, top)
    def _(j):
        v = v_ref[pl.ds(j * wide, wide), :, head].reshape(keys, HEAD_SIZE)
        both = widened(v)
        for t, s in enumerate(scores(j)):
            old = peak_ref[t][:, 0:1]
            peak = jnp.maximum(old, jnp.max(s, axis=1, keepdims=True))
            acc_ref[t] = acc_ref[t] * jnp.exp2(old - peak) + weigh(s, peak, both)
            peak_ref[t] = jnp.broadcast_to(peak, peak_ref.shape[1:])

    outs = [(acc_ref[t][:, :HEAD_SIZE] / acc_ref[t][:, HEAD_SIZE:]).astype(BF) for t in range(chains)]
    o_ref[:, here] = jnp.concatenate(
        [out[h * rows : (h + 1) * rows] for out in outs for h in range(per_chain)], axis=1
    )


def layer_kernel(
    n, inner, chunks, groups, ways, steps_out,
    x_in, maps_in, z_in, steps_in, rates_in, skip_in, tapx_in, tapm_in, gain_in, w_ref, q_in, k_ref, v_ref,
    o_ref, attn_ref,
    x_ref, maps_ref, z_ref, steps_ref, rates_ref, skip_ref, tapx_ref, tapm_ref, gain_ref, q_ref, in_sem,
    xc_ref, bc_ref, cum_ref, cumt_ref, dt_ref, ent_ref, kbuf, vbuf,
    halo_x, halo_m, ext, wbuf, srow, rrow, ein, eout, pbuf,
    halo_send, halo_recv, own_sem, kz_send, vz_send, kr_send, vr_send, k_recv, v_recv,
    s_send, s_recv, e_send, e_recv, p_send, p_recv,
    y_ref, nbuf, turned, peak_ref, acc_ref,
    w_buf, lhs, mine, out1, in1, out2, in2,
    w_sem, send1, recv1, send2, recv2,
):
    outer = n // inner
    c = lax.axis_index("ctx")
    hi = lax.div(c, inner)
    lo = lax.rem(c, inner)
    rows, xcols = x_ref.shape
    mcols = maps_ref.shape[1]
    heads = steps_ref.shape[0]
    head_dim = xcols // heads
    nstate = mcols // groups // 2
    width = srow.shape[3]
    part = width * chunks

    def remote(src, dst, send, recv, place):
        return pltpu.make_async_remote_copy(
            src_ref=src, dst_ref=dst, send_sem=send, recv_sem=recv,
            device_id={"ctx": place}, device_id_type=MESH,
        )

    inputs = [
        pltpu.make_async_copy(src, dst, in_sem.at[i])
        for i, (src, dst) in enumerate((
            (x_in, x_ref), (maps_in, maps_ref), (steps_in, steps_ref), (rates_in, rates_ref),
            (tapx_in, tapx_ref), (tapm_in, tapm_ref), (skip_in, skip_ref), (gain_in, gain_ref),
            (q_in, q_ref), (z_in, z_ref),
        ))
    ]
    for copy in inputs:
        copy.start()

    tp = 2 * ways
    me = lax.axis_index("tp")
    core = lax.rem(me, 2)
    place = lax.div(me, 2)
    partner = place * 2 + 1 - core
    share = o_ref.shape[0]
    half = ways * share
    out_width = w_buf.shape[2]

    def w_copy(j):
        cols = pl.ds(pl.multiple_of(j * out_width, out_width), out_width)
        return pltpu.make_async_copy(w_ref.at[:, cols], w_buf.at[j], w_sem.at[j])

    barrier = pltpu.get_barrier_semaphore()
    for away in range(1, tp):
        pl.semaphore_signal(
            barrier, inc=1, device_id={"tp": lax.rem(me + away, tp)}, device_id_type=MESH
        )
    for away in range(1, n):
        pl.semaphore_signal(
            barrier, inc=1, device_id={"ctx": lax.rem(c + away, n)}, device_id_type=MESH
        )
    for copy in inputs[:2]:
        copy.wait()
    pl.semaphore_wait(barrier, n + tp - 2)

    up = lax.rem(c + inner, n)
    nxt = lax.rem(c + 1, n)

    def kv_up(src_k, src_v, block):
        return (
            remote(src_k, kbuf.at[block], kz_send.at[block], k_recv.at[block], up),
            remote(src_v, vbuf.at[block], vz_send.at[block], v_recv.at[block], up),
        )

    def kv_row(src_k, src_v, block, peer):
        place = hi * inner + peer
        return (
            remote(src_k, kbuf.at[block], kr_send.at[block, peer], k_recv.at[block], place),
            remote(src_v, vbuf.at[block], vr_send.at[block, peer], v_recv.at[block], place),
        )

    def halo_copies():
        return (
            remote(x_ref.at[pl.ds(rows - 16, 16)], halo_x, halo_send.at[0], halo_recv.at[0], nxt),
            remote(maps_ref.at[pl.ds(rows - 16, 16)], halo_m, halo_send.at[1], halo_recv.at[1], nxt),
        )

    @pl.when(c < n - 1)
    def _():
        for copy in halo_copies():
            copy.start()

    @pl.when(hi < outer - 1)
    def _():
        for copy in kv_up(k_ref, v_ref, c):
            copy.start()

    for away in range(1, inner):
        peer = lax.rem(lo + away, inner)

        @pl.when(peer > lo)
        def _():
            for copy in kv_row(k_ref, v_ref, c, peer):
                copy.start()

    own = (
        pltpu.make_async_copy(k_ref, kbuf.at[c], own_sem.at[0]),
        pltpu.make_async_copy(v_ref, vbuf.at[c], own_sem.at[1]),
    )
    for copy in own:
        copy.start()

    for j in range(steps_out):
        w_copy(j).start()
    for copy in inputs[2:]:
        copy.wait()

    raw = steps_ref[...]
    dt = jnp.maximum(raw, 0.0) + jnp.log1p(jnp.exp(-jnp.abs(raw)))
    square = (heads, heads)
    rates = jnp.sum(
        jnp.where(
            lax.broadcasted_iota(jnp.int32, square, 0) == lax.broadcasted_iota(jnp.int32, square, 1),
            jnp.broadcast_to(rates_ref[...], square), 0.0,
        ),
        axis=1, keepdims=True,
    )
    cum = dt * -jnp.exp(rates)
    lane = lax.broadcasted_iota(jnp.int32, cum.shape, 1)
    reach = 1
    while reach < rows:
        cum = cum + jnp.where(lane >= reach, pltpu.roll(cum, reach, 1), 0.0)
        reach *= 2
    cum_ref[...] = cum
    dt_ref[...] = dt
    per_group = heads // groups
    last = cum[:, rows - 1 : rows]
    tail = (jnp.exp(last - cum) * dt).T
    cum_t = cum.T
    for g in range(groups):
        cumt_ref[g] = cum_t[:, g * per_group : (g + 1) * per_group]
    end_decay = jnp.exp(cum_t[rows - 1 : rows])

    @pl.when(c == 0)
    def _():
        halo_x[...] = jnp.zeros_like(halo_x)
        halo_m[...] = jnp.zeros_like(halo_m)

    @pl.when(c > 0)
    def _():
        for copy in halo_copies():
            copy.wait_recv()

    taps = tapx_ref.shape[0]
    step = 256

    def conv(src, halo, tap_ref, dst, cols):
        ext[0:8, :] = halo[:, cols].astype(F32)[8:16]
        ext[8 : 8 + rows, :] = src[:, cols].astype(F32)
        tap = tap_ref[:, cols].astype(F32)
        total = jnp.zeros((rows, step), F32)
        for k in range(taps):
            total = total + tap[k : k + 1] * ext[pl.ds(9 - taps + k, rows), :]
        dst[:, cols] = silu(total).astype(BF)

    for j in range(mcols // step):
        conv(maps_ref, halo_m, tapm_ref, bc_ref, slice(j * step, (j + 1) * step))
    for j in range(xcols // step):
        conv(x_ref, halo_x, tapx_ref, xc_ref, slice(j * step, (j + 1) * step))

    def pass_on(k):
        block = lax.rem(c - k * inner + n, n)

        @pl.when(hi >= k)
        def _():
            for copy in kv_up(kbuf.at[block], vbuf.at[block], block):
                copy.wait_recv()

            @pl.when(hi < outer - 1)
            def _():
                for copy in kv_up(kbuf.at[block], vbuf.at[block], block):
                    copy.start()

            for away in range(1, inner):
                for copy in kv_row(kbuf.at[block], vbuf.at[block], block, lax.rem(lo + away, inner)):
                    copy.start()

    if outer > 1:
        pass_on(1)

    for p in range(heads // 2):
        cols = slice(2 * p * head_dim, 2 * (p + 1) * head_dim)
        weight = pair_lanes(
            tail[:, 2 * p : 2 * p + 1], tail[:, 2 * p + 1 : 2 * p + 2], rows, head_dim
        )
        wbuf[:, cols] = (weight * xc_ref[:, cols].astype(F32)).astype(BF)
        at = 2 * p * head_dim
        srow[at // part, (at % part) // width, nstate : nstate + 16,
             at % width : at % width + 2 * head_dim] = pair_lanes(
            end_decay[:, 2 * p : 2 * p + 1], end_decay[:, 2 * p + 1 : 2 * p + 2], 16, head_dim
        ).astype(BF)
    group_cols = xcols // groups
    for m in range(inner):
        for ch in range(chunks):
            at = m * part + ch * width
            g = at // group_cols
            b_map = bc_ref[:, g * 2 * nstate : g * 2 * nstate + nstate]
            srow[m, ch, 0:nstate] = lax.dot_general(
                b_map, wbuf[:, at : at + width], (((0,), (0,)), ((), ())),
                preferred_element_type=F32,
            ).astype(BF)

    def s_copy(peer, ch):
        return remote(
            srow.at[peer, ch], rrow.at[lo, ch], s_send.at[peer, ch], s_recv.at[lo, ch],
            hi * inner + peer,
        )

    def s_arrival(peer, ch):
        return remote(
            srow.at[peer, ch], rrow.at[peer, ch], s_send.at[peer, ch], s_recv.at[peer, ch],
            hi * inner + peer,
        )

    for ch in range(chunks):
        for away in range(1, inner):
            s_copy(lax.rem(lo + away, inner), ch).start()
        rrow[lo, ch] = srow[lo, ch]

    if outer > 2:
        pass_on(2)
    for g in range(groups):
        mix_inside(g, groups, xc_ref, bc_ref, cum_ref, cumt_ref, dt_ref, skip_ref, y_ref)
    for k in range(3, outer):
        pass_on(k)

    for copy in own:
        copy.wait()
    for k in range(outer):
        for away in range(1, inner):
            peer = lax.rem(lo + away, inner)
            theirs = lax.rem(hi - k + outer, outer) * inner + peer

            @pl.when((hi >= k) if k else (peer < lo))
            def _():
                for copy in kv_row(kbuf.at[theirs], vbuf.at[theirs], theirs, peer):
                    copy.wait_recv()

    steps_attn = q_ref.shape[1] * rows // HEAD_SIZE // (acc_ref.shape[0] * acc_ref.shape[1])
    early = jnp.minimum(steps_attn // 2, jnp.maximum(hi - 1, 0))

    @pl.loop(0, c + 1)
    def _(j):
        turned[j] = kbuf[j].T

    @pl.loop(0, early)
    def _(i):
        attend_step(i, c, q_ref, turned, vbuf, attn_ref, peak_ref, acc_ref)

    def e_copy(ch):
        return remote(eout.at[ch], ein.at[ch], e_send.at[ch], e_recv.at[ch], up)

    def p_copy(peer, ch):
        return remote(
            pbuf.at[peer, ch], ent_ref.at[lo, ch], p_send.at[peer, ch], p_recv.at[lo, ch],
            hi * inner + peer,
        )

    def p_arrival(peer, ch):
        return remote(
            pbuf.at[peer, ch], ent_ref.at[peer, ch], p_send.at[peer, ch], p_recv.at[peer, ch],
            hi * inner + peer,
        )

    for ch in range(chunks):
        for away in range(1, inner):
            s_arrival(lax.rem(lo + away, inner), ch).wait_recv()

        @pl.when(hi == 0)
        def _():
            ein[ch] = jnp.zeros_like(ein[ch])

        @pl.when(hi > 0)
        def _():
            e_copy(ch).wait_recv()

        state = ein[ch].astype(F32)
        for m in range(inner):
            pbuf[m, ch] = state.astype(BF)
            state = rrow[m, ch, nstate : nstate + 16].astype(F32)[0:1] * state + rrow[
                m, ch, 0:nstate
            ].astype(F32)
        eout[ch] = state.astype(BF)

        @pl.when(hi < outer - 1)
        def _():
            e_copy(ch).start()

        for away in range(1, inner):
            p_copy(lax.rem(lo + away, inner), ch).start()
        ent_ref[lo, ch] = pbuf[lo, ch]

    for ch in range(chunks):
        for away in range(1, inner):
            p_arrival(lax.rem(lo + away, inner), ch).wait_recv()

    for g in range(groups):
        mix_finish(g, groups, bc_ref, cumt_ref, ent_ref, z_ref, gain_ref, nbuf, y_ref)

    for x in range(ways):
        theirs = pl.multiple_of((2 * x + 1 - core) * share, share)
        ours = pl.multiple_of((2 * x + core) * share, share)
        lhs[x * share : (x + 1) * share] = nbuf[pl.ds(theirs, share)]
        lhs[half + x * share : half + (x + 1) * share] = nbuf[pl.ds(ours, share)]

    def copy1(j):
        return pltpu.make_async_remote_copy(
            src_ref=out1.at[j], dst_ref=in1.at[j], send_sem=send1.at[j], recv_sem=recv1.at[j],
            device_id={"tp": partner}, device_id_type=MESH,
        )

    def copy2(j, away):
        other = lax.rem(place + away, ways)
        return pltpu.make_async_remote_copy(
            src_ref=out2.at[j, other], dst_ref=in2.at[j, ways - away],
            send_sem=send2.at[j, away], recv_sem=recv2.at[j, ways - away],
            device_id={"tp": other * 2 + core}, device_id_type=MESH,
        )

    def arrival2(j, away):
        other = lax.rem(place + away, ways)
        return pltpu.make_async_remote_copy(
            src_ref=out2.at[j, other], dst_ref=in2.at[j, away],
            send_sem=send2.at[j, away], recv_sem=recv2.at[j, away],
            device_id={"tp": other * 2 + core}, device_id_type=MESH,
        )

    def multiply(j):
        w_copy(j).wait()
        part = jnp.dot(lhs[...], w_buf[j], preferred_element_type=F32).astype(BF)
        out1[j] = part[:half]
        mine[j] = part[half:]
        copy1(j).start()

    def across(j):
        copy1(j).wait_recv()
        total = mine[j].astype(F32) + in1[j].astype(F32)
        for x in range(ways):
            out2[j, x] = total[x * share : (x + 1) * share].astype(BF)
        for away in range(1, ways):
            copy2(j, away).start()

    def finish(j):
        here = pl.ds(pl.multiple_of(place * share, share), share)
        total = mine[j, here].astype(F32) + in1[j, here].astype(F32)
        for away in range(1, ways):
            arrival2(j, away).wait_recv()
            total = total + in2[j, away].astype(F32)
        o_ref[:, pl.ds(pl.multiple_of(j * out_width, out_width), out_width)] = total.astype(BF)

    @pl.loop(0, steps_out)
    def _(j):
        multiply(j)

        @pl.when(j >= 1)
        def _():
            across(j - 1)

    across(steps_out - 1)

    @pl.loop(early, steps_attn)
    def _(i):
        attend_step(i, c, q_ref, turned, vbuf, attn_ref, peak_ref, acc_ref)

    @pl.loop(0, steps_out)
    def _(j):
        finish(j)

    for j in range(steps_out):
        copy1(j).wait_send()
        for away in range(1, ways):
            copy2(j, away).wait_send()

    for k in range(outer):
        block = lax.rem(c - k * inner + n, n)
        for away in range(1, inner):
            peer = lax.rem(lo + away, inner)

            @pl.when((hi >= k) if k else (peer > lo))
            def _():
                for copy in kv_row(kbuf.at[block], vbuf.at[block], block, peer):
                    copy.wait_send()

        @pl.when((hi >= k) & (hi < outer - 1))
        def _():
            for copy in kv_up(kbuf.at[block], vbuf.at[block], block):
                copy.wait_send()

    for ch in range(chunks):
        for away in range(1, inner):
            peer = lax.rem(lo + away, inner)
            s_copy(peer, ch).wait_send()
            p_copy(peer, ch).wait_send()

        @pl.when(hi < outer - 1)
        def _():
            e_copy(ch).wait_send()

    @pl.when(c < n - 1)
    def _():
        for copy in halo_copies():
            copy.wait_send()


def hand_over_kernel(a_ref, b_ref, a_out, b_out, sem):
    copies = (
        pltpu.make_async_copy(a_ref, a_out, sem.at[0]),
        pltpu.make_async_copy(b_ref, b_out, sem.at[1]),
    )
    for copy in copies:
        copy.start()
    for copy in copies:
        copy.wait()


def hand_over(pair):
    hbm = pl.BlockSpec(memory_space=pl.ANY)
    return pl.pallas_call(
        hand_over_kernel,
        out_shape=tuple(jax.ShapeDtypeStruct(a.shape, a.dtype) for a in pair),
        in_specs=[hbm, hbm],
        out_specs=(hbm, hbm),
        scratch_shapes=[pltpu.SemaphoreType.DMA((2,))],
        name="hand_over",
    )(*pair)


def per_device(
    n, tp, ssm_inputs, state_maps, ssm_gates, time_steps, log_rates, skip_gain, conv_inputs, conv_maps,
    norm_gain, out_weight, queries, attention_keys, values,
):
    rows, xcols = ssm_inputs.shape
    groups = state_maps.shape[1]
    heads = log_rates.shape[0]
    maps = state_maps.reshape(rows, -1)
    mcols = maps.shape[1]
    taps = conv_inputs.shape[0]
    nstate = mcols // groups // 2
    depth, cols = out_weight.shape
    inner = 2 if n <= 8 else 8
    part = xcols // inner
    chunks = max(1, part // 512)
    width = part // chunks
    ways = tp // 2
    share = rows // tp
    half = ways * share
    out_width = 512
    steps = cols // out_width
    kvcols = attention_keys.shape[1]
    vm = pl.BlockSpec(memory_space=pltpu.VMEM)
    hbm = pl.BlockSpec(memory_space=pl.ANY)
    dma = pltpu.SemaphoreType.DMA
    return hand_over(pl.pallas_call(
        functools.partial(layer_kernel, n, inner, chunks, groups, ways, steps),
        out_shape=(
            jax.ShapeDtypeStruct((share, cols), BF),
            jax.ShapeDtypeStruct(queries.shape, BF),
        ),
        in_specs=[hbm] * 13,
        out_specs=(vm, vm),
        scratch_shapes=[
            pltpu.VMEM((rows, xcols), BF),
            pltpu.VMEM((rows, mcols), BF),
            pltpu.VMEM((rows, xcols), BF),
            pltpu.VMEM((heads, rows), F32),
            pltpu.VMEM((1, heads), F32),
            pltpu.VMEM((1, heads), F32),
            pltpu.VMEM((taps, xcols), BF),
            pltpu.VMEM((taps, mcols), BF),
            pltpu.VMEM((1, xcols), F32),
            pltpu.VMEM(queries.shape, BF),
            dma((10,)),
            pltpu.VMEM((rows, xcols), BF),
            pltpu.VMEM((rows, mcols), BF),
            pltpu.VMEM((heads, rows), F32),
            pltpu.VMEM((groups, rows, heads // groups), F32),
            pltpu.VMEM((heads, rows), F32),
            pltpu.VMEM((inner, chunks, nstate, width), BF),
            pltpu.VMEM((n, rows, kvcols), BF),
            pltpu.VMEM((n, rows, kvcols), BF),
            pltpu.VMEM((16, xcols), BF),
            pltpu.VMEM((16, mcols), BF),
            pltpu.VMEM((rows + 8, 256), F32),
            pltpu.VMEM((rows, xcols), BF),
            pltpu.VMEM((inner, chunks, nstate + 16, width), BF),
            pltpu.VMEM((inner, chunks, nstate + 16, width), BF),
            pltpu.VMEM((chunks, nstate, width), BF),
            pltpu.VMEM((chunks, nstate, width), BF),
            pltpu.VMEM((inner, chunks, nstate, width), BF),
            dma((2,)), dma((2,)), dma((2,)),
            dma((n,)), dma((n,)), dma((n, inner)), dma((n, inner)), dma((n,)), dma((n,)),
            dma((inner, chunks)), dma((inner, chunks)),
            dma((chunks,)), dma((chunks,)),
            dma((inner, chunks)), dma((inner, chunks)),
            pltpu.VMEM((rows, xcols), F32),
            pltpu.VMEM((rows, xcols), BF),
            pltpu.VMEM((n, kvcols, rows), BF),
            pltpu.VMEM((2, 2 * rows, 128), F32),
            pltpu.VMEM((2, 2 * rows, 2 * HEAD_SIZE), F32),
            pltpu.VMEM((steps, depth, out_width), BF),
            pltpu.VMEM((rows, depth), BF),
            pltpu.VMEM((steps, half, out_width), BF),
            pltpu.VMEM((steps, half, out_width), BF),
            pltpu.VMEM((steps, half, out_width), BF),
            pltpu.VMEM((steps, ways, share, out_width), BF),
            pltpu.VMEM((steps, ways, share, out_width), BF),
            dma((steps,)), dma((steps,)), dma((steps,)),
            dma((steps, ways)), dma((steps, ways)),
        ],
        compiler_params=pltpu.CompilerParams(
            collective_id=0, has_side_effects=True, vmem_limit_bytes=58 * 2**20
        ),
        name="layer",
    )(
        ssm_inputs, maps, ssm_gates, time_steps, log_rates.reshape(1, heads),
        skip_gain.reshape(1, heads), conv_inputs, conv_maps.reshape(taps, mcols),
        norm_gain.reshape(1, xcols), out_weight, queries, attention_keys, values,
    ))


def solution(mesh):
    placed = (
        P("ctx", "tp"),
        P("ctx", "tp", None),
        P("ctx", "tp"),
        P("tp", "ctx"),
        P("tp"),
        P("tp"),
        P(None, "tp"),
        P(None, "tp", None),
        P("tp"),
        P("tp", None),
        P("ctx", "tp"),
        P("ctx", "tp"),
        P("ctx", "tp"),
    )
    return jax.shard_map(
        functools.partial(per_device, mesh.shape["ctx"], mesh.shape["tp"]),
        mesh=mesh,
        in_specs=placed,
        out_specs=(P(("ctx", "tp"), None), P("ctx", "tp")),
        check_vma=False,
    )
```

```python
import functools

import jax
import jax.numpy as jnp
from jax import lax
from jax.experimental import pallas as pl
from jax.experimental.pallas import tpu as pltpu
from jax.sharding import PartitionSpec as P

HEAD_SIZE = 128
SHARED = 8
MESH = pl.DeviceIdType.MESH
LOG2E = 1.4426950408889634
BF = jnp.bfloat16
F32 = jnp.float32


def pair_lanes(col_a, col_b, rows, head_dim):
    lane = lax.broadcasted_iota(jnp.int32, (rows, 2 * head_dim), 1)
    return jnp.where(
        lane < head_dim,
        jnp.broadcast_to(col_a, (rows, 2 * head_dim)),
        jnp.broadcast_to(col_b, (rows, 2 * head_dim)),
    )


def silu(v):
    return v / (1.0 + jnp.exp(-v))


def mix_inside(g, groups, xc_ref, bc_ref, cum_ref, cumt_ref, dt_ref, skip_ref, y_ref):
    rows = xc_ref.shape[0]
    cols = xc_ref.shape[1] // groups
    per_group = cum_ref.shape[0] // groups
    head_dim = cols // per_group
    nstate = bc_ref.shape[1] // groups // 2
    b_map = bc_ref[:, 2 * g * nstate : (2 * g + 1) * nstate]
    c_map = bc_ref[:, (2 * g + 1) * nstate : (2 * g + 2) * nstate]
    products = lax.dot_general(
        c_map, b_map, (((1,), (1,)), ((), ())), preferred_element_type=F32
    )
    tok = lax.broadcasted_iota(jnp.int32, (rows, rows), 0)
    src = lax.broadcasted_iota(jnp.int32, (rows, rows), 1)
    products = jnp.where(tok >= src, products, 0.0)
    cum_t = cumt_ref[g]
    lane = lax.broadcasted_iota(jnp.int32, (rows, 2 * head_dim), 1)
    for p in range(per_group // 2):
        at = g * cols + 2 * p * head_dim
        span = slice(at, at + 2 * head_dim)
        xp = xc_ref[:, span]
        inner = []
        for h in (2 * p, 2 * p + 1):
            row = slice(g * per_group + h, g * per_group + h + 1)
            gap = jnp.minimum(cum_t[:, h : h + 1] - cum_ref[row, :], 0.0)
            mix = (products * jnp.exp(gap) * dt_ref[row, :]).astype(BF)
            inner.append(jnp.dot(mix, xp, preferred_element_type=F32))
        h = g * per_group + 2 * p
        skip = pair_lanes(skip_ref[0:1, h : h + 1], skip_ref[0:1, h + 1 : h + 2], 1, head_dim)
        y_ref[:, span] = jnp.where(lane < head_dim, inner[0], inner[1]) + skip * xp.astype(F32)


def mix_finish(g, groups, bc_ref, cumt_ref, ent_ref, z_ref, gain_ref, out_ref, y_ref):
    rows = z_ref.shape[0]
    cols = z_ref.shape[1] // groups
    per_group = cumt_ref.shape[2]
    head_dim = cols // per_group
    nstate = bc_ref.shape[1] // groups // 2
    chunks, width = ent_ref.shape[1], ent_ref.shape[3]
    part = chunks * width
    c_map = bc_ref[:, (2 * g + 1) * nstate : (2 * g + 2) * nstate]
    rise = jnp.exp(cumt_ref[g])
    square = jnp.zeros((rows, 2 * head_dim), F32)
    for p in range(per_group // 2):
        at = g * cols + 2 * p * head_dim
        span = slice(at, at + 2 * head_dim)
        inside = at % width
        carried = jnp.dot(
            c_map, ent_ref[at // part, (at % part) // width, :, inside : inside + 2 * head_dim],
            preferred_element_type=F32,
        )
        y = y_ref[:, span] + carried * pair_lanes(
            rise[:, 2 * p : 2 * p + 1], rise[:, 2 * p + 1 : 2 * p + 2], rows, head_dim
        )
        u = y * silu(z_ref[:, span].astype(F32))
        y_ref[:, span] = u
        square = square + u * u
    scale = lax.rsqrt(jnp.sum(square, axis=1, keepdims=True) * (1.0 / cols) + 1e-5)
    own = slice(g * cols, (g + 1) * cols)
    out_ref[:, own] = (y_ref[:, own] * scale * gain_ref[0:1, own]).astype(BF)


def attend_step(i, c, q_ref, k_ref, v_ref, o_ref, peak_ref, acc_ref):
    rows = q_ref.shape[0]
    wide = min(4, k_ref.shape[0])
    keys = wide * rows
    chains, tall = acc_ref.shape[:2]
    together = chains * tall // rows
    per_chain = tall // rows
    per_kv = SHARED // together
    span = together * HEAD_SIZE
    head = pl.ds(pl.multiple_of(lax.div(i, per_kv) * HEAD_SIZE, HEAD_SIZE), HEAD_SIZE)
    here = pl.ds(pl.multiple_of(i * span, span), span)
    q_all = q_ref[:, here]
    qs = [
        jnp.concatenate(
            [q_all[:, h * HEAD_SIZE : (h + 1) * HEAD_SIZE]
             for h in range(t * per_chain, (t + 1) * per_chain)], axis=0
        )
        for t in range(chains)
    ]
    scale = HEAD_SIZE**-0.5 * LOG2E

    def scores(j):
        k = jnp.concatenate([k_ref[j * wide + b, head, :] for b in range(wide)], axis=1)
        return [jnp.dot(q, k, preferred_element_type=F32) * scale for q in qs]

    def weigh(s, peak, both):
        return jnp.dot(jnp.exp2(s - peak).astype(BF), both, preferred_element_type=F32)

    def widened(v):
        return jnp.concatenate([v, jnp.ones((keys, HEAD_SIZE), BF)], axis=1)

    top = lax.div(c, wide)
    offset = lax.rem(c, wide) * rows
    tok = lax.rem(lax.broadcasted_iota(jnp.int32, (tall, keys), 0), rows) + offset
    pos = lax.broadcasted_iota(jnp.int32, (tall, keys), 1)
    allowed = pos <= tok
    v = v_ref[pl.ds(top * wide, wide), :, head].reshape(keys, HEAD_SIZE)
    held = lax.broadcasted_iota(jnp.int32, (keys, HEAD_SIZE), 0) < offset + rows
    both = widened(jnp.where(held, v, jnp.zeros_like(v)))
    for t, s in enumerate(scores(top)):
        s = jnp.where(allowed, s, -1e30)
        peak = jnp.max(s, axis=1, keepdims=True)
        acc_ref[t] = weigh(s, peak, both)
        peak_ref[t] = jnp.broadcast_to(peak, peak_ref.shape[1:])

    @pl.loop(0, top)
    def _(j):
        v = v_ref[pl.ds(j * wide, wide), :, head].reshape(keys, HEAD_SIZE)
        both = widened(v)
        for t, s in enumerate(scores(j)):
            old = peak_ref[t][:, 0:1]
            peak = jnp.maximum(old, jnp.max(s, axis=1, keepdims=True))
            acc_ref[t] = acc_ref[t] * jnp.exp2(old - peak) + weigh(s, peak, both)
            peak_ref[t] = jnp.broadcast_to(peak, peak_ref.shape[1:])

    outs = [(acc_ref[t][:, :HEAD_SIZE] / acc_ref[t][:, HEAD_SIZE:]).astype(BF) for t in range(chains)]
    o_ref[:, here] = jnp.concatenate(
        [out[h * rows : (h + 1) * rows] for out in outs for h in range(per_chain)], axis=1
    )


def layer_kernel(
    n, inner, chunks, groups, ways, steps_out,
    x_in, maps_in, z_in, steps_in, rates_in, skip_in, tapx_in, tapm_in, gain_in, w_ref, q_in, k_ref, v_ref,
    o_ref, attn_ref,
    x_ref, maps_ref, z_ref, steps_ref, rates_ref, skip_ref, tapx_ref, tapm_ref, gain_ref, q_ref, in_sem,
    xc_ref, bc_ref, cum_ref, cumt_ref, dt_ref, ent_ref, kbuf, vbuf,
    halo_x, halo_m, ext, wbuf, srow, rrow, ein, eout, pbuf,
    halo_send, halo_recv, own_sem, kz_send, vz_send, kr_send, vr_send, k_recv, v_recv,
    s_send, s_recv, e_send, e_recv, p_send, p_recv,
    y_ref, nbuf, turned, peak_ref, acc_ref,
    w_buf, lhs, mine, out1, in1, out2, in2,
    w_sem, send1, recv1, send2, recv2,
):
    outer = n // inner
    c = lax.axis_index("ctx")
    hi = lax.div(c, inner)
    lo = lax.rem(c, inner)
    rows, xcols = x_ref.shape
    mcols = maps_ref.shape[1]
    heads = steps_ref.shape[0]
    head_dim = xcols // heads
    nstate = mcols // groups // 2
    width = srow.shape[3]
    part = width * chunks

    def remote(src, dst, send, recv, place):
        return pltpu.make_async_remote_copy(
            src_ref=src, dst_ref=dst, send_sem=send, recv_sem=recv,
            device_id={"ctx": place}, device_id_type=MESH,
        )

    inputs = [
        pltpu.make_async_copy(src, dst, in_sem.at[i])
        for i, (src, dst) in enumerate((
            (x_in, x_ref), (maps_in, maps_ref), (steps_in, steps_ref), (rates_in, rates_ref),
            (tapx_in, tapx_ref), (tapm_in, tapm_ref), (skip_in, skip_ref), (gain_in, gain_ref),
            (q_in, q_ref), (z_in, z_ref),
        ))
    ]
    for copy in inputs:
        copy.start()

    tp = 2 * ways
    me = lax.axis_index("tp")
    core = lax.rem(me, 2)
    place = lax.div(me, 2)
    partner = place * 2 + 1 - core
    share = o_ref.shape[0]
    half = ways * share
    out_width = w_buf.shape[2]

    def w_copy(j):
        cols = pl.ds(pl.multiple_of(j * out_width, out_width), out_width)
        return pltpu.make_async_copy(w_ref.at[:, cols], w_buf.at[j], w_sem.at[j])

    barrier = pltpu.get_barrier_semaphore()
    for away in range(1, tp):
        pl.semaphore_signal(
            barrier, inc=1, device_id={"tp": lax.rem(me + away, tp)}, device_id_type=MESH
        )
    for away in range(1, n):
        pl.semaphore_signal(
            barrier, inc=1, device_id={"ctx": lax.rem(c + away, n)}, device_id_type=MESH
        )
    for copy in inputs[:2]:
        copy.wait()
    pl.semaphore_wait(barrier, n + tp - 2)

    up = lax.rem(c + inner, n)
    nxt = lax.rem(c + 1, n)

    def kv_up(src_k, src_v, block):
        return (
            remote(src_k, kbuf.at[block], kz_send.at[block], k_recv.at[block], up),
            remote(src_v, vbuf.at[block], vz_send.at[block], v_recv.at[block], up),
        )

    def kv_row(src_k, src_v, block, peer):
        place = hi * inner + peer
        return (
            remote(src_k, kbuf.at[block], kr_send.at[block, peer], k_recv.at[block], place),
            remote(src_v, vbuf.at[block], vr_send.at[block, peer], v_recv.at[block], place),
        )

    def halo_copies():
        return (
            remote(x_ref.at[pl.ds(rows - 16, 16)], halo_x, halo_send.at[0], halo_recv.at[0], nxt),
            remote(maps_ref.at[pl.ds(rows - 16, 16)], halo_m, halo_send.at[1], halo_recv.at[1], nxt),
        )

    @pl.when(c < n - 1)
    def _():
        for copy in halo_copies():
            copy.start()

    @pl.when(hi < outer - 1)
    def _():
        for copy in kv_up(k_ref, v_ref, c):
            copy.start()

    for away in range(1, inner):
        peer = lax.rem(lo + away, inner)

        @pl.when(peer > lo)
        def _():
            for copy in kv_row(k_ref, v_ref, c, peer):
                copy.start()

    own = (
        pltpu.make_async_copy(k_ref, kbuf.at[c], own_sem.at[0]),
        pltpu.make_async_copy(v_ref, vbuf.at[c], own_sem.at[1]),
    )
    for copy in own:
        copy.start()

    for j in range(steps_out):
        w_copy(j).start()
    for copy in inputs[2:]:
        copy.wait()

    raw = steps_ref[...]
    dt = jnp.maximum(raw, 0.0) + jnp.log1p(jnp.exp(-jnp.abs(raw)))
    square = (heads, heads)
    rates = jnp.sum(
        jnp.where(
            lax.broadcasted_iota(jnp.int32, square, 0) == lax.broadcasted_iota(jnp.int32, square, 1),
            jnp.broadcast_to(rates_ref[...], square), 0.0,
        ),
        axis=1, keepdims=True,
    )
    cum = dt * -jnp.exp(rates)
    lane = lax.broadcasted_iota(jnp.int32, cum.shape, 1)
    reach = 1
    while reach < rows:
        cum = cum + jnp.where(lane >= reach, pltpu.roll(cum, reach, 1), 0.0)
        reach *= 2
    cum_ref[...] = cum
    dt_ref[...] = dt
    per_group = heads // groups
    last = cum[:, rows - 1 : rows]
    tail = (jnp.exp(last - cum) * dt).T
    cum_t = cum.T
    for g in range(groups):
        cumt_ref[g] = cum_t[:, g * per_group : (g + 1) * per_group]
    end_decay = jnp.exp(cum_t[rows - 1 : rows])

    @pl.when(c == 0)
    def _():
        halo_x[...] = jnp.zeros_like(halo_x)
        halo_m[...] = jnp.zeros_like(halo_m)

    @pl.when(c > 0)
    def _():
        for copy in halo_copies():
            copy.wait_recv()

    taps = tapx_ref.shape[0]
    step = 256

    def conv(src, halo, tap_ref, dst, cols):
        ext[0:8, :] = halo[:, cols].astype(F32)[8:16]
        ext[8 : 8 + rows, :] = src[:, cols].astype(F32)
        tap = tap_ref[:, cols].astype(F32)
        total = jnp.zeros((rows, step), F32)
        for k in range(taps):
            total = total + tap[k : k + 1] * ext[pl.ds(9 - taps + k, rows), :]
        dst[:, cols] = silu(total).astype(BF)

    for j in range(mcols // step):
        conv(maps_ref, halo_m, tapm_ref, bc_ref, slice(j * step, (j + 1) * step))
    for j in range(xcols // step):
        conv(x_ref, halo_x, tapx_ref, xc_ref, slice(j * step, (j + 1) * step))

    def pass_on(k):
        block = lax.rem(c - k * inner + n, n)

        @pl.when(hi >= k)
        def _():
            for copy in kv_up(kbuf.at[block], vbuf.at[block], block):
                copy.wait_recv()

            @pl.when(hi < outer - 1)
            def _():
                for copy in kv_up(kbuf.at[block], vbuf.at[block], block):
                    copy.start()

            for away in range(1, inner):
                for copy in kv_row(kbuf.at[block], vbuf.at[block], block, lax.rem(lo + away, inner)):
                    copy.start()

    if outer > 1:
        pass_on(1)

    for p in range(heads // 2):
        cols = slice(2 * p * head_dim, 2 * (p + 1) * head_dim)
        weight = pair_lanes(
            tail[:, 2 * p : 2 * p + 1], tail[:, 2 * p + 1 : 2 * p + 2], rows, head_dim
        )
        wbuf[:, cols] = (weight * xc_ref[:, cols].astype(F32)).astype(BF)
        at = 2 * p * head_dim
        srow[at // part, (at % part) // width, nstate : nstate + 16,
             at % width : at % width + 2 * head_dim] = pair_lanes(
            end_decay[:, 2 * p : 2 * p + 1], end_decay[:, 2 * p + 1 : 2 * p + 2], 16, head_dim
        ).astype(BF)
    group_cols = xcols // groups
    for m in range(inner):
        for ch in range(chunks):
            at = m * part + ch * width
            g = at // group_cols
            b_map = bc_ref[:, g * 2 * nstate : g * 2 * nstate + nstate]
            srow[m, ch, 0:nstate] = lax.dot_general(
                b_map, wbuf[:, at : at + width], (((0,), (0,)), ((), ())),
                preferred_element_type=F32,
            ).astype(BF)

    def s_copy(peer, ch):
        return remote(
            srow.at[peer, ch], rrow.at[lo, ch], s_send.at[peer, ch], s_recv.at[lo, ch],
            hi * inner + peer,
        )

    def s_arrival(peer, ch):
        return remote(
            srow.at[peer, ch], rrow.at[peer, ch], s_send.at[peer, ch], s_recv.at[peer, ch],
            hi * inner + peer,
        )

    for ch in range(chunks):
        for away in range(1, inner):
            s_copy(lax.rem(lo + away, inner), ch).start()
        rrow[lo, ch] = srow[lo, ch]

    if outer > 2:
        pass_on(2)
    for g in range(groups):
        mix_inside(g, groups, xc_ref, bc_ref, cum_ref, cumt_ref, dt_ref, skip_ref, y_ref)
    for k in range(3, outer):
        pass_on(k)

    for copy in own:
        copy.wait()
    for k in range(outer):
        for away in range(1, inner):
            peer = lax.rem(lo + away, inner)
            theirs = lax.rem(hi - k + outer, outer) * inner + peer

            @pl.when((hi >= k) if k else (peer < lo))
            def _():
                for copy in kv_row(kbuf.at[theirs], vbuf.at[theirs], theirs, peer):
                    copy.wait_recv()

    steps_attn = q_ref.shape[1] * rows // HEAD_SIZE // (acc_ref.shape[0] * acc_ref.shape[1])
    early = jnp.minimum(steps_attn // 2, jnp.maximum(hi - 1, 0))

    @pl.loop(0, c + 1)
    def _(j):
        turned[j] = kbuf[j].T

    @pl.loop(0, early)
    def _(i):
        attend_step(i, c, q_ref, turned, vbuf, attn_ref, peak_ref, acc_ref)

    def e_copy(ch):
        return remote(eout.at[ch], ein.at[ch], e_send.at[ch], e_recv.at[ch], up)

    def p_copy(peer, ch):
        return remote(
            pbuf.at[peer, ch], ent_ref.at[lo, ch], p_send.at[peer, ch], p_recv.at[lo, ch],
            hi * inner + peer,
        )

    def p_arrival(peer, ch):
        return remote(
            pbuf.at[peer, ch], ent_ref.at[peer, ch], p_send.at[peer, ch], p_recv.at[peer, ch],
            hi * inner + peer,
        )

    for ch in range(chunks):
        for away in range(1, inner):
            s_arrival(lax.rem(lo + away, inner), ch).wait_recv()

        @pl.when(hi == 0)
        def _():
            ein[ch] = jnp.zeros_like(ein[ch])

        @pl.when(hi > 0)
        def _():
            e_copy(ch).wait_recv()

        state = ein[ch].astype(F32)
        for m in range(inner):
            pbuf[m, ch] = state.astype(BF)
            state = rrow[m, ch, nstate : nstate + 16].astype(F32)[0:1] * state + rrow[
                m, ch, 0:nstate
            ].astype(F32)
        eout[ch] = state.astype(BF)

        @pl.when(hi < outer - 1)
        def _():
            e_copy(ch).start()

        for away in range(1, inner):
            p_copy(lax.rem(lo + away, inner), ch).start()
        ent_ref[lo, ch] = pbuf[lo, ch]

    for ch in range(chunks):
        for away in range(1, inner):
            p_arrival(lax.rem(lo + away, inner), ch).wait_recv()

    for g in range(groups):
        mix_finish(g, groups, bc_ref, cumt_ref, ent_ref, z_ref, gain_ref, nbuf, y_ref)

    for x in range(ways):
        theirs = pl.multiple_of((2 * x + 1 - core) * share, share)
        ours = pl.multiple_of((2 * x + core) * share, share)
        lhs[x * share : (x + 1) * share] = nbuf[pl.ds(theirs, share)]
        lhs[half + x * share : half + (x + 1) * share] = nbuf[pl.ds(ours, share)]

    def copy1(j):
        return pltpu.make_async_remote_copy(
            src_ref=out1.at[j], dst_ref=in1.at[j], send_sem=send1.at[j], recv_sem=recv1.at[j],
            device_id={"tp": partner}, device_id_type=MESH,
        )

    def copy2(j, away):
        other = lax.rem(place + away, ways)
        return pltpu.make_async_remote_copy(
            src_ref=out2.at[j, other], dst_ref=in2.at[j, ways - away],
            send_sem=send2.at[j, away], recv_sem=recv2.at[j, ways - away],
            device_id={"tp": other * 2 + core}, device_id_type=MESH,
        )

    def arrival2(j, away):
        other = lax.rem(place + away, ways)
        return pltpu.make_async_remote_copy(
            src_ref=out2.at[j, other], dst_ref=in2.at[j, away],
            send_sem=send2.at[j, away], recv_sem=recv2.at[j, away],
            device_id={"tp": other * 2 + core}, device_id_type=MESH,
        )

    def multiply(j):
        w_copy(j).wait()
        part = jnp.dot(lhs[...], w_buf[j], preferred_element_type=F32).astype(BF)
        out1[j] = part[:half]
        mine[j] = part[half:]
        copy1(j).start()

    def across(j):
        copy1(j).wait_recv()
        total = mine[j].astype(F32) + in1[j].astype(F32)
        for x in range(ways):
            out2[j, x] = total[x * share : (x + 1) * share].astype(BF)
        for away in range(1, ways):
            copy2(j, away).start()

    def finish(j):
        here = pl.ds(pl.multiple_of(place * share, share), share)
        total = mine[j, here].astype(F32) + in1[j, here].astype(F32)
        for away in range(1, ways):
            arrival2(j, away).wait_recv()
            total = total + in2[j, away].astype(F32)
        o_ref[:, pl.ds(pl.multiple_of(j * out_width, out_width), out_width)] = total.astype(BF)

    @pl.loop(0, steps_out)
    def _(j):
        multiply(j)

        @pl.when(j >= 1)
        def _():
            across(j - 1)

    across(steps_out - 1)

    @pl.loop(early, steps_attn)
    def _(i):
        attend_step(i, c, q_ref, turned, vbuf, attn_ref, peak_ref, acc_ref)

    @pl.loop(0, steps_out)
    def _(j):
        finish(j)

    for j in range(steps_out):
        copy1(j).wait_send()
        for away in range(1, ways):
            copy2(j, away).wait_send()

    for k in range(outer):
        block = lax.rem(c - k * inner + n, n)
        for away in range(1, inner):
            peer = lax.rem(lo + away, inner)

            @pl.when((hi >= k) if k else (peer > lo))
            def _():
                for copy in kv_row(kbuf.at[block], vbuf.at[block], block, peer):
                    copy.wait_send()

        @pl.when((hi >= k) & (hi < outer - 1))
        def _():
            for copy in kv_up(kbuf.at[block], vbuf.at[block], block):
                copy.wait_send()

    for ch in range(chunks):
        for away in range(1, inner):
            peer = lax.rem(lo + away, inner)
            s_copy(peer, ch).wait_send()
            p_copy(peer, ch).wait_send()

        @pl.when(hi < outer - 1)
        def _():
            e_copy(ch).wait_send()

    @pl.when(c < n - 1)
    def _():
        for copy in halo_copies():
            copy.wait_send()


def hand_over_kernel(a_ref, b_ref, a_out, b_out, sem):
    copies = (
        pltpu.make_async_copy(a_ref, a_out, sem.at[0]),
        pltpu.make_async_copy(b_ref, b_out, sem.at[1]),
    )
    for copy in copies:
        copy.start()
    for copy in copies:
        copy.wait()


def hand_over(pair):
    hbm = pl.BlockSpec(memory_space=pl.ANY)
    vm = pl.BlockSpec(memory_space=pltpu.VMEM)
    return pl.pallas_call(
        hand_over_kernel,
        out_shape=tuple(jax.ShapeDtypeStruct(a.shape, a.dtype) for a in pair),
        in_specs=[vm, vm],
        out_specs=(hbm, hbm),
        scratch_shapes=[pltpu.SemaphoreType.DMA((2,))],
        name="hand_over",
    )(*pair)


def per_device(
    n, tp, ssm_inputs, state_maps, ssm_gates, time_steps, log_rates, skip_gain, conv_inputs, conv_maps,
    norm_gain, out_weight, queries, attention_keys, values,
):
    rows, xcols = ssm_inputs.shape
    groups = state_maps.shape[1]
    heads = log_rates.shape[0]
    maps = state_maps.reshape(rows, -1)
    mcols = maps.shape[1]
    taps = conv_inputs.shape[0]
    nstate = mcols // groups // 2
    depth, cols = out_weight.shape
    inner = 2 if n <= 8 else 8
    part = xcols // inner
    chunks = max(1, part // 512)
    width = part // chunks
    ways = tp // 2
    share = rows // tp
    half = ways * share
    out_width = 512
    steps = cols // out_width
    kvcols = attention_keys.shape[1]
    vm = pl.BlockSpec(memory_space=pltpu.VMEM)
    hbm = pl.BlockSpec(memory_space=pl.ANY)
    dma = pltpu.SemaphoreType.DMA
    return hand_over(pl.pallas_call(
        functools.partial(layer_kernel, n, inner, chunks, groups, ways, steps),
        out_shape=(
            jax.ShapeDtypeStruct((share, cols), BF),
            jax.ShapeDtypeStruct(queries.shape, BF),
        ),
        in_specs=[hbm] * 13,
        out_specs=(vm, vm),
        scratch_shapes=[
            pltpu.VMEM((rows, xcols), BF),
            pltpu.VMEM((rows, mcols), BF),
            pltpu.VMEM((rows, xcols), BF),
            pltpu.VMEM((heads, rows), F32),
            pltpu.VMEM((1, heads), F32),
            pltpu.VMEM((1, heads), F32),
            pltpu.VMEM((taps, xcols), BF),
            pltpu.VMEM((taps, mcols), BF),
            pltpu.VMEM((1, xcols), F32),
            pltpu.VMEM(queries.shape, BF),
            dma((10,)),
            pltpu.VMEM((rows, xcols), BF),
            pltpu.VMEM((rows, mcols), BF),
            pltpu.VMEM((heads, rows), F32),
            pltpu.VMEM((groups, rows, heads // groups), F32),
            pltpu.VMEM((heads, rows), F32),
            pltpu.VMEM((inner, chunks, nstate, width), BF),
            pltpu.VMEM((n, rows, kvcols), BF),
            pltpu.VMEM((n, rows, kvcols), BF),
            pltpu.VMEM((16, xcols), BF),
            pltpu.VMEM((16, mcols), BF),
            pltpu.VMEM((rows + 8, 256), F32),
            pltpu.VMEM((rows, xcols), BF),
            pltpu.VMEM((inner, chunks, nstate + 16, width), BF),
            pltpu.VMEM((inner, chunks, nstate + 16, width), BF),
            pltpu.VMEM((chunks, nstate, width), BF),
            pltpu.VMEM((chunks, nstate, width), BF),
            pltpu.VMEM((inner, chunks, nstate, width), BF),
            dma((2,)), dma((2,)), dma((2,)),
            dma((n,)), dma((n,)), dma((n, inner)), dma((n, inner)), dma((n,)), dma((n,)),
            dma((inner, chunks)), dma((inner, chunks)),
            dma((chunks,)), dma((chunks,)),
            dma((inner, chunks)), dma((inner, chunks)),
            pltpu.VMEM((rows, xcols), F32),
            pltpu.VMEM((rows, xcols), BF),
            pltpu.VMEM((n, kvcols, rows), BF),
            pltpu.VMEM((2, 2 * rows, 128), F32),
            pltpu.VMEM((2, 2 * rows, 2 * HEAD_SIZE), F32),
            pltpu.VMEM((steps, depth, out_width), BF),
            pltpu.VMEM((rows, depth), BF),
            pltpu.VMEM((steps, half, out_width), BF),
            pltpu.VMEM((steps, half, out_width), BF),
            pltpu.VMEM((steps, half, out_width), BF),
            pltpu.VMEM((steps, ways, share, out_width), BF),
            pltpu.VMEM((steps, ways, share, out_width), BF),
            dma((steps,)), dma((steps,)), dma((steps,)),
            dma((steps, ways)), dma((steps, ways)),
        ],
        compiler_params=pltpu.CompilerParams(
            collective_id=0, has_side_effects=True, vmem_limit_bytes=58 * 2**20
        ),
        name="layer",
    )(
        ssm_inputs, maps, ssm_gates, time_steps, log_rates.reshape(1, heads),
        skip_gain.reshape(1, heads), conv_inputs, conv_maps.reshape(taps, mcols),
        norm_gain.reshape(1, xcols), out_weight, queries, attention_keys, values,
    ))


def solution(mesh):
    placed = (
        P("ctx", "tp"),
        P("ctx", "tp", None),
        P("ctx", "tp"),
        P("tp", "ctx"),
        P("tp"),
        P("tp"),
        P(None, "tp"),
        P(None, "tp", None),
        P("tp"),
        P("tp", None),
        P("ctx", "tp"),
        P("ctx", "tp"),
        P("ctx", "tp"),
    )
    return jax.shard_map(
        functools.partial(per_device, mesh.shape["ctx"], mesh.shape["tp"]),
        mesh=mesh,
        in_specs=placed,
        out_specs=(P(("ctx", "tp"), None), P("ctx", "tp")),
        check_vma=False,
    )
```
